128 devices in a mesh: gx: 8 (over z, core), gy: 16 (over x, y).
Axes of the slice: x: 4, y: 4, z: 4, core: 2. Of those that a mesh axis runs over, the one named last changes fastest.
Arguments:
- view_tiles: bfloat16 [49152, 32, 128], P(('gx', 'gy')), may hold values from 0.19921875 to 5
- tile_owner: int32 [49152], P(('gx', 'gy')), may hold values from 0 to 127, as said below
- tile_offset: int32 [49152], P(('gx', 'gy')), may hold values from 0 to 383, as said below
- estimate: float32 [512, 512, 128], P('gx', 'gy'), may hold values from 0.5 to 2
- spread_taps: float32 [6, 3, 31], replicated, may hold values from 0.05 to 1
Outputs:
- updated: float32 [512, 512, 128], P('gx', 'gy')
The draws below stay inside these ranges and needn't reach their ends.
Inputs may be any that keep to these rules, and one draw needn't show every extreme that they name: `tile_owner`: the owner of every tile is the device at most one step away along gx and at most one step along gy from the device that holds the tile, counted around the device grid; no device sends more than 64 tiles to one owner, and every device sends exactly 64 to some owner; every owner receives exactly 384 tiles in all. `tile_offset`: over the tiles of one owner the offsets are all of 0 to 383, each once.
All inputs are finite; a program needn't handle non-finite values.
Results may differ from the reference program's by a relative error of at most 0.001.
Values may be sent and summed in bfloat16 or wider, within the bound.
A program may use at most 128 MiB of HBM per device.

```python
import math
import jax
import jax.numpy as jnp
from jax import lax

VIEWS = 6
TAPS = 31
CX = 64
CY = 32
DEPTH = 128
TILES_DEV = 384
NX = 512
NY = 512
N_GX = 8
N_GY = 16
DEVICES = 128


def route_table(key):
    order = jax.random.permutation(jax.random.fold_in(key, 11), 9)
    base = jnp.array([4, 4, 4, 4, 2, 2, 2, 1, 1], jnp.int32) * (CX // 4)
    counts = base[order]
    ends = jnp.cumsum(counts)
    places = jax.random.permutation(jax.random.fold_in(key, 12), TILES_DEV)
    source_keys = jax.random.split(jax.random.fold_in(key, 13), DEVICES)

    def shuffle(subkey):
        return jax.random.permutation(subkey, TILES_DEV)
    picks = jax.vmap(shuffle)(source_keys).astype(jnp.int32)
    group = jnp.sum((picks[:, :, None] >= ends[None, None, :]).astype(jnp.int32), axis=2)
    step_row = group // 3 - 1
    step_col = group % 3 - 1
    source = jnp.arange(DEVICES, dtype=jnp.int32)[:, None]
    owner_row = (source // N_GY + step_row + N_GX) % N_GX
    owner_col = (source % N_GY + step_col + N_GY) % N_GY
    owner = owner_row * N_GY + owner_col
    offset = (places[picks] + 5 * owner) % TILES_DEV
    return (owner.reshape(-1).astype(jnp.int32), offset.reshape(-1).astype(jnp.int32))


def draw_tile_owner(key, part):
    return route_table(key)[0]


def draw_tile_offset(key, part):
    return route_table(key)[1]


def levels(own_key, dims, pieces, smallest, top_value):
    def one(position, shards_of):
        steps = jax.random.uniform(jax.random.fold_in(jax.random.fold_in(own_key, 6), position), (shards_of,), jnp.float32, smallest / len(pieces), top_value / len(pieces))
        return jnp.repeat(jnp.exp(steps), dims[position] // shards_of).reshape((-1,) + (1,) * (len(dims) - position - 1))

    factor_of = one(*pieces[0])
    for cut in pieces[1:]:
        factor_of = factor_of * one(*cut)
    return factor_of


def setup_inputs(seed: int = 0) -> dict:
    splits = jax.random.split(jax.random.key(seed), 6)
    return {
        "view_tiles": jnp.clip(jnp.exp(math.log(5.0) - 3.2227897 * jax.random.uniform(splits[0], (DEVICES * TILES_DEV, CY, DEPTH), jnp.float32) ** levels(splits[0], (DEVICES * TILES_DEV, CY, DEPTH), ((0, 128),), -0.2, 0.2)), 0.19921875, 5.0).astype(jnp.bfloat16),
        "tile_owner": draw_tile_owner(jax.random.fold_in(splits[5], 71), 0),
        "tile_offset": draw_tile_offset(jax.random.fold_in(splits[5], 71), 0),
        "estimate": jnp.clip(jnp.exp(math.log(2.0) - 1.3862944 * jax.random.uniform(splits[3], (NX, NY, DEPTH), jnp.float32) ** levels(splits[3], (NX, NY, DEPTH), ((0, 8), (1, 16)), -0.2, 0.2)), 0.5, 2.0),
        "spread_taps": jnp.clip(jnp.exp(jax.random.uniform(splits[4], (VIEWS, 3, TAPS), jnp.float32, math.log(0.05), math.log(1.0))), 0.05, 1.0),
    }


def blur_axis(volume, taps, axis):
    shape_list = [1, 1, 1]
    shape_list[axis] = TAPS
    weights = taps.reshape(1, 1, shape_list[0], shape_list[1], shape_list[2])
    padding = [(0, 0), (0, 0), (0, 0)]
    padding[axis] = (TAPS // 2, TAPS // 2)
    result = lax.conv_general_dilated(volume[None, None], weights, (1, 1, 1), padding, precision=lax.Precision.HIGHEST)
    return result[0, 0]


def project(volume, kernel):
    out_vol = blur_axis(volume, kernel[2], 2)
    out_vol = blur_axis(out_vol, kernel[1], 1)
    return blur_axis(out_vol, kernel[0], 0)


def reference(view_tiles, tile_owner, tile_offset, estimate, spread_taps):
    kernel = spread_taps / jnp.sum(spread_taps, axis=2, keepdims=True)
    owner_row = tile_owner // N_GY
    owner_col = tile_owner % N_GY
    view_index = tile_offset // CX
    row_index = owner_row * CX + tile_offset % CX
    view_data = jnp.zeros((VIEWS, NX, N_GY, CY, DEPTH), jnp.bfloat16)
    view_data = view_data.at[view_index, row_index, owner_col].set(view_tiles)
    view_data = view_data.reshape(VIEWS, NX, NY, DEPTH)

    def per_view(items):
        observed, taps = items
        forward_blur = project(estimate, taps)
        ratio_volume = observed.astype(jnp.float32) / forward_blur
        return project(ratio_volume, taps[:, ::-1])

    backward = lax.map(per_view, (view_data, kernel))
    return estimate * (jnp.sum(backward, axis=0) / VIEWS)
```

```python
import jax
import jax.numpy as jnp
from jax import lax
from jax.experimental import pallas as pl
from jax.experimental.pallas import tpu as pltpu
from jax.sharding import PartitionSpec as P

MESH = pl.DeviceIdType.MESH
F32, BF16, I32 = jnp.float32, jnp.bfloat16, jnp.int32

VIEWS, TAPS = 6, 31
ROWS, COLS, DEPTH = 64, 32, 128
TILES = 384
HALO = 16
XROWS, XCOLS = ROWS + 2 * HALO, COLS + 2 * HALO
SLOTS = 64
OWN = 4
ORDER = (5, 3, 2, 0, 8, 6, 1, 7)
BANDS = XROWS // 16
TILE_BANDS = ROWS // 16


def dot(a, b):
    return jnp.dot(a, b, preferred_element_type=F32)


def dot_nt(a, b):
    return lax.dot_general(a, b, (((1,), (1,)), ((), ())), preferred_element_type=F32)


def iota(shape, dim):
    return lax.broadcasted_iota(I32, shape, dim)


def onehot(mask):
    return jnp.where(mask, 1.0, 0.0).astype(BF16)


def shifted_rows(row, rows, shift):
    wide = jnp.broadcast_to(row, (rows, row.shape[1]))
    return pltpu.roll(wide, shift, 1, stride=1, stride_axis=0)


def lanes(a, b):
    return jnp.concatenate([a, b], axis=1)


def kernel(
    nx, ny,
    taps_ref, owner_ref, offset_ref, est_hbm, tiles_hbm,
    out_ref,
    est_v, tiles_v, packed, arrived, ext, blurred, recip, quot, back_rows,
    center, side_out, side_in, row_out, row_in,
    kpad, row_fwd, row_bwd, col_fwd, col_bwd, depth_fwd, depth_bwd,
    index_v, index_s, slot_v, slot_s, label_out, label_in,
    load_sem, index_sem,
    halo_send, halo_recv, tile_send, tile_recv, label_send, label_recv,
    side_send, side_recv, row_send, row_recv,
):
    gx, gy = lax.axis_index("gx"), lax.axis_index("gy")

    def device(dx, dy):
        return (lax.rem(gx + dx + nx, nx), lax.rem(gy + dy + ny, ny))

    def step_of(group):
        return group // 3 - 1, group % 3 - 1

    load_est = pltpu.make_async_copy(est_hbm, est_v, load_sem.at[0])
    load_tiles = pltpu.make_async_copy(tiles_hbm, tiles_v, load_sem.at[1])
    load_est.start()
    load_tiles.start()

    barrier = pltpu.get_barrier_semaphore()
    for group in ORDER:
        pl.semaphore_signal(barrier, inc=1, device_id=device(*step_of(group)), device_id_type=MESH)

    load_est.wait()
    zero_row = jnp.zeros((XCOLS, DEPTH), BF16)
    ext[0] = zero_row
    ext[XROWS - 1] = zero_row
    ext[HALO:HALO + ROWS, HALO:HALO + COLS, :] = est_v[...].astype(BF16)
    pl.semaphore_wait(barrier, len(ORDER))

    def part(step, size):
        if step > 0:
            return (size, size + HALO), (0, HALO)
        if step < 0:
            return (HALO, 2 * HALO), (size + HALO, size + 2 * HALO)
        return (HALO, HALO + size), (HALO, HALO + size)

    halo_copies = []
    for group in ORDER:
        dx, dy = step_of(group)
        (r0, r1), (s0, s1) = part(dx, ROWS)
        if dx > 0:
            r0, s0 = r0 + 1, s0 + 1
        if dx < 0:
            r1, s1 = r1 - 1, s1 - 1
        (c0, c1), (d0, d1) = part(dy, COLS)
        copy = pltpu.make_async_remote_copy(
            src_ref=ext.at[r0:r1, c0:c1, :],
            dst_ref=ext.at[s0:s1, d0:d1, :],
            send_sem=halo_send.at[group],
            recv_sem=halo_recv.at[group],
            device_id=device(dx, dy),
            device_id_type=MESH,
        )
        copy.start()
        halo_copies.append(copy)

    owner = owner_ref[...]
    shift = ny.bit_length() - 1

    def wrapped(d, n):
        return jnp.where(d == 0, 1, jnp.where(d == 1, 2, jnp.where(d == 1 - n, 2, 0)))

    group_of = wrapped((owner >> shift) - gx, nx) * 3 + wrapped((owner & (ny - 1)) - gy, ny)
    members = jnp.where(iota((16, TILES), 0) == group_of, 1.0, 0.0)
    before = onehot(iota((TILES, TILES), 0) < iota((TILES, TILES), 1))
    rank = jnp.sum(members * dot(members.astype(BF16), before), axis=0, keepdims=True)
    place = group_of * 128 + rank.astype(I32)
    picks = onehot(iota((9 * 128, TILES), 0) == place)
    number = iota((8, TILES), 1)
    row = iota((8, TILES), 0)
    offset = jnp.broadcast_to(offset_ref[...], (8, TILES))
    digits = jnp.where(row == 0, number >> 4, jnp.where(row == 1, number & 15, jnp.where(
        row == 2, offset >> 4, jnp.where(row == 3, offset & 15, 1))))
    found = dot_nt(digits.astype(F32).astype(BF16), picks)
    source = jnp.clip((found[0:1] * 16.0 + found[1:2]).astype(I32), 0, TILES - 1)
    label = (found[2:3] * 16.0 + found[3:4] + (found[4:5] - 1.0) * 1024.0).astype(I32)
    index_v[...] = jnp.zeros_like(index_v)
    for group in range(9):
        index_v[group:group + 1, :] = source[:, group * 128:(group + 1) * 128]
        label_out[group] = jnp.broadcast_to(label[:, group * 128:(group + 1) * 128], (8, 128))
    load_index = pltpu.make_async_copy(index_v, index_s, index_sem.at[0])
    load_index.start()
    label_copies = []
    for group in ORDER:
        copy = pltpu.make_async_remote_copy(
            src_ref=label_out.at[group],
            dst_ref=label_in.at[group],
            send_sem=label_send.at[group],
            recv_sem=label_recv.at[group],
            device_id=device(*step_of(group)),
            device_id_type=MESH,
        )
        copy.start()
        label_copies.append(copy)
    label_in[OWN] = label_out[OWN]

    load_index.wait()
    load_tiles.wait()
    tile_copies = []
    for group in ORDER:
        def pack(r, carry, group=group):
            packed[group * SLOTS + r] = tiles_v[index_s[group, r]]
            return carry

        lax.fori_loop(0, SLOTS, pack, 0, unroll=8)
        copy = pltpu.make_async_remote_copy(
            src_ref=packed.at[group * SLOTS:(group + 1) * SLOTS],
            dst_ref=arrived.at[group * SLOTS:(group + 1) * SLOTS],
            send_sem=tile_send.at[group],
            recv_sem=tile_recv.at[group],
            device_id=device(*step_of(group)),
            device_id_type=MESH,
        )
        copy.start()
        tile_copies.append(copy)

    def keep(r, carry):
        arrived[OWN * SLOTS + r] = tiles_v[index_s[OWN, r]]
        return carry

    lax.fori_loop(0, SLOTS, keep, 0, unroll=8)

    kpad[...] = jnp.zeros_like(kpad)
    kpad[:, 0:3, 0:TAPS] = taps_ref[...]
    spread = onehot((iota((256, 16), 0) >> 4) == iota((256, 16), 1))
    spread_wide = onehot((iota((768, 128), 0) >> 4) == iota((768, 128), 1))
    same = (iota((256, 256), 0) & 15) == (iota((256, 256), 1) & 15)
    eye = onehot(iota((128, 128), 0) == iota((128, 128), 1))
    depth_fwd[...] = jnp.zeros_like(depth_fwd)
    depth_bwd[...] = jnp.zeros_like(depth_bwd)
    for v in range(VIEWS):
        raw = kpad[v][0:3]
        norm = raw / jnp.sum(raw, axis=1, keepdims=True)
        rows_band = shifted_rows(norm[0:1], 16, 1).astype(BF16)
        wide = dot(spread, rows_band).astype(BF16)
        for d in range(3):
            fwd = dot_nt(wide, spread_wide[256 * d:256 * (d + 1)])
            row_fwd[v, :, 256 * d:256 * (d + 1)] = jnp.where(same, fwd, 0.0).astype(BF16)
            tall = dot_nt(spread_wide[256 * d:256 * (d + 1)], rows_band).astype(BF16)
            bwd = dot_nt(tall, spread)
            row_bwd[v, :, 256 * (2 - d):256 * (3 - d)] = jnp.where(same, bwd, 0.0).astype(BF16)
        cols_band = shifted_rows(norm[1:2], COLS, 1)
        col_fwd[v * COLS:(v + 1) * COLS, :] = cols_band.astype(BF16)
        long = lanes(norm[2:3], jnp.zeros((1, 128), F32))
        depth_t = shifted_rows(long, DEPTH, 128 - TAPS // 2)[:, 128:256].astype(BF16)
        at = slice(128 * (v % 2), 128 * (v % 2) + 128)
        depth_bwd[v // 2, at, at] = depth_t
        depth_fwd[v // 2, at, at] = dot_nt(eye, depth_t).astype(BF16)
    col_bwd[...] = dot_nt(eye[0:XCOLS], col_fwd[...]).astype(BF16)

    for copy in halo_copies:
        copy.wait_recv()

    def clear(edge, rows, cols):
        @pl.when(edge)
        def _():
            ext[rows, cols, :] = jnp.zeros((rows.stop - rows.start, cols.stop - cols.start, DEPTH), BF16)

    every_row, every_col = slice(0, XROWS), slice(0, XCOLS)
    clear(gx == 0, slice(0, HALO), every_col)
    clear(gx == nx - 1, slice(XROWS - HALO, XROWS), every_col)
    clear(gy == 0, every_row, slice(0, HALO))
    clear(gy == ny - 1, every_row, slice(XCOLS - HALO, XCOLS))

    def columns(p, carry):
        a = 2 * p
        both = lanes(ext[a], ext[a + 1])
        out = dot(col_fwd[:, 0:XCOLS], both).astype(BF16)
        blurred[a] = out[:, 0:128].reshape(VIEWS, COLS, DEPTH)
        blurred[a + 1] = out[:, 128:256].reshape(VIEWS, COLS, DEPTH)
        return carry

    lax.fori_loop(0, XROWS // 2, columns, 0)

    def rows_depth(n, carry):
        band, pair = n // 3, n % 3
        first = pl.multiple_of(band * 16, 16)
        parts = []
        for e in range(2):
            block = blurred[pl.ds(first, 48), 2 * pair + e]
            both = lanes(block[:, 0:16].reshape(768, DEPTH), block[:, 16:32].reshape(768, DEPTH))
            parts.append(dot(row_fwd[2 * pair + e], both).astype(BF16))
        for h in range(2):
            both = lanes(parts[0][:, 128 * h:128 * h + 128], parts[1][:, 128 * h:128 * h + 128])
            inverse = 1.0 / dot(both, depth_fwd[pair])
            for e in range(2):
                recip[2 * pair + e, pl.ds(first, 16), 16 * h:16 * h + 16, :] = inverse[
                    :, 128 * e:128 * e + 128].reshape(16, 16, DEPTH)
        return carry

    lax.fori_loop(0, TILE_BANDS * 3, rows_depth, 0)

    for copy in label_copies:
        copy.wait_recv()
    labels = jnp.concatenate([label_in[group][0:1] for group in range(9)], axis=1)
    where_is = onehot(iota((TILES, 9 * 128), 0) == labels)
    place_no = iota((8, 9 * 128), 1)
    place_digits = jnp.where(iota((8, 9 * 128), 0) == 0, place_no >> 7, place_no & 127)
    got = dot_nt(place_digits.astype(F32).astype(BF16), where_is)
    slots = jnp.clip((got[0:1] * float(SLOTS) + got[1:2]).astype(I32), 0, 9 * SLOTS - 1)
    slot_v[...] = jnp.zeros_like(slot_v)
    for n in range(3):
        slot_v[n:n + 1, :] = slots[:, 128 * n:128 * (n + 1)]
    load_slots = pltpu.make_async_copy(slot_v, slot_s, index_sem.at[1])
    load_slots.start()
    load_slots.wait()
    for copy in tile_copies:
        copy.wait_recv()

    side_copies, row_copies = [], []
    for band in range(BANDS):
        if band < TILE_BANDS:
            def quotients(pair, carry, band=band):
                tiles = []
                for i in range(16):
                    halves = []
                    for e in range(2):
                        at = slot_s[pair, 64 * e + 16 * band + i]
                        value = arrived[at].astype(F32) * recip[2 * pair + e, 16 * band + i]
                        halves.append(value.astype(BF16))
                    tiles.append(lanes(halves[0], halves[1]))
                out = dot(jnp.concatenate(tiles, axis=0), depth_bwd[pair]).astype(BF16)
                for e in range(2):
                    quot[2 * pair + e, 16 * band:16 * band + 16] = out[
                        :, 128 * e:128 * e + 128].reshape(16, COLS, DEPTH)
                return carry

            lax.fori_loop(0, 3, quotients, 0)
        s0, s1 = max(0, band - 2), min(TILE_BANDS - 1, band)
        w0, w1 = 256 * (2 - (band - s0)), 256 * (3 - (band - s1))

        def rows_back(v, carry, s0=s0, s1=s1, w0=w0, w1=w1):
            block = quot[v, 16 * s0:16 * (s1 + 1)]
            both = lanes(block[:, 0:16].reshape(w1 - w0, DEPTH), block[:, 16:32].reshape(w1 - w0, DEPTH))
            out = dot(row_bwd[v, :, w0:w1], both).astype(BF16)
            back_rows[:, v, 0:16, :] = out[:, 0:128].reshape(16, 16, DEPTH)
            back_rows[:, v, 16:32, :] = out[:, 128:256].reshape(16, 16, DEPTH)
            return carry

        lax.fori_loop(0, VIEWS, rows_back, 0)

        def cols_back(p, carry, band=band):
            both = lanes(back_rows[2 * p].reshape(VIEWS * COLS, DEPTH), back_rows[2 * p + 1].reshape(VIEWS * COLS, DEPTH))
            out = dot(col_bwd[...], both)
            for e in range(2):
                one = out[:, 128 * e:128 * e + 128]
                side_out[band, 0, 2 * p + e] = one[0:HALO].astype(BF16)
                side_out[band, 1, 2 * p + e] = one[HALO + COLS:XCOLS].astype(BF16)
                mid = one[HALO:HALO + COLS]
                if 1 <= band <= TILE_BANDS:
                    center[16 * (band - 1) + 2 * p + e] = mid
                else:
                    row_out[band // (BANDS - 1), 2 * p + e] = mid.astype(BF16)
            return carry

        lax.fori_loop(0, 8, cols_back, 0)
        dx = -1 if band == 0 else 1 if band == BANDS - 1 else 0
        for side in range(2):
            copy = pltpu.make_async_remote_copy(
                src_ref=side_out.at[band, side],
                dst_ref=side_in.at[band, side],
                send_sem=side_send.at[band, side],
                recv_sem=side_recv.at[band, side],
                device_id=device(dx, 2 * side - 1),
                device_id_type=MESH,
            )
            copy.start()
            side_copies.append(copy)
        if dx != 0:
            end = band // (BANDS - 1)
            copy = pltpu.make_async_remote_copy(
                src_ref=row_out.at[end],
                dst_ref=row_in.at[end],
                send_sem=row_send.at[end],
                recv_sem=row_recv.at[end],
                device_id=device(dx, 0),
                device_id_type=MESH,
            )
            copy.start()
            row_copies.append(copy)

    for copy in side_copies + row_copies:
        copy.wait_recv()

    from_right, from_left = gy != ny - 1, gy != 0
    for c in range(TILE_BANDS):
        rows = slice(16 * c, 16 * c + 16)

        def sides(band, inside):
            low = side_in[band, 1].astype(F32)
            high = side_in[band, 0].astype(F32)
            return jnp.concatenate([
                jnp.where(jnp.logical_and(from_left, inside), low, 0.0),
                jnp.where(jnp.logical_and(from_right, inside), high, 0.0),
            ], axis=1)

        total = center[rows] + sides(c + 1, True)
        if c == 0:
            inside = gx != 0
            total = total + sides(BANDS - 1, inside) + jnp.where(inside, row_in[1].astype(F32), 0.0)
        if c == TILE_BANDS - 1:
            inside = gx != nx - 1
            total = total + sides(0, inside) + jnp.where(inside, row_in[0].astype(F32), 0.0)
        out_ref[rows] = total

    for copy in halo_copies + label_copies + tile_copies + side_copies + row_copies:
        copy.wait_send()


def body(view_tiles, tile_owner, tile_offset, estimate, spread_taps):
    nx, ny = lax.axis_size("gx"), lax.axis_size("gy")
    vmem = pl.BlockSpec(memory_space=pltpu.VMEM)
    anywhere = pl.BlockSpec(memory_space=pl.ANY)
    dma = pltpu.SemaphoreType.DMA
    total = pl.pallas_call(
        lambda *refs: kernel(nx, ny, *refs),
        out_shape=jax.ShapeDtypeStruct((ROWS, COLS, DEPTH), F32),
        in_specs=[vmem, vmem, vmem, anywhere, anywhere],
        out_specs=vmem,
        scratch_shapes=[
            pltpu.VMEM((ROWS, COLS, DEPTH), F32),
            pltpu.VMEM((TILES, COLS, DEPTH), BF16),
            pltpu.VMEM((9 * SLOTS, COLS, DEPTH), BF16),
            pltpu.VMEM((9 * SLOTS, COLS, DEPTH), BF16),
            pltpu.VMEM((XROWS, XCOLS, DEPTH), BF16),
            pltpu.VMEM((XROWS, VIEWS, COLS, DEPTH), BF16),
            pltpu.VMEM((VIEWS, ROWS, COLS, DEPTH), F32),
            pltpu.VMEM((VIEWS, ROWS, COLS, DEPTH), BF16),
            pltpu.VMEM((16, VIEWS, COLS, DEPTH), BF16),
            pltpu.VMEM((ROWS, COLS, DEPTH), F32),
            pltpu.VMEM((BANDS, 2, 16, HALO, DEPTH), BF16),
            pltpu.VMEM((BANDS, 2, 16, HALO, DEPTH), BF16),
            pltpu.VMEM((2, 16, COLS, DEPTH), BF16),
            pltpu.VMEM((2, 16, COLS, DEPTH), BF16),
            pltpu.VMEM((VIEWS, 8, 128), F32),
            pltpu.VMEM((VIEWS, 256, 768), BF16),
            pltpu.VMEM((VIEWS, 256, 768), BF16),
            pltpu.VMEM((VIEWS * COLS, 128), BF16),
            pltpu.VMEM((XCOLS, VIEWS * COLS), BF16),
            pltpu.VMEM((VIEWS // 2, 256, 256), BF16),
            pltpu.VMEM((VIEWS // 2, 256, 256), BF16),
            pltpu.VMEM((16, 128), I32),
            pltpu.SMEM((16, 128), I32),
            pltpu.VMEM((8, 128), I32),
            pltpu.SMEM((8, 128), I32),
            pltpu.VMEM((9, 8, 128), I32),
            pltpu.VMEM((9, 8, 128), I32),
            dma((2,)), dma((2,)),
            dma((9,)), dma((9,)), dma((9,)), dma((9,)), dma((9,)), dma((9,)),
            dma((BANDS, 2)), dma((BANDS, 2)), dma((2,)), dma((2,)),
        ],
        compiler_params=pltpu.CompilerParams(
            collective_id=0, has_side_effects=True, vmem_limit_bytes=56 * 1024 * 1024
        ),
        name="richardson_lucy",
    )(spread_taps, tile_owner.reshape(1, TILES), tile_offset.reshape(1, TILES), estimate, view_tiles)
    return estimate * (total / VIEWS)


def solution(mesh):
    placed = (
        P(("gx", "gy"), None, None),
        P(("gx", "gy")),
        P(("gx", "gy")),
        P("gx", "gy", None),
        P(),
    )
    return jax.shard_map(
        body, mesh=mesh, in_specs=placed, out_specs=P("gx", "gy", None), check_vma=False
    )
```

```python
import jax
import jax.numpy as jnp
from jax import lax
from jax.experimental import pallas as pl
from jax.experimental.pallas import tpu as pltpu
from jax.sharding import PartitionSpec as P

MESH = pl.DeviceIdType.MESH
F32, BF16, I32 = jnp.float32, jnp.bfloat16, jnp.int32

VIEWS, TAPS = 6, 31
ROWS, COLS, DEPTH = 64, 32, 128
TILES = 384
HALO = 16
XROWS, XCOLS = ROWS + 2 * HALO, COLS + 2 * HALO
SLOTS = 64
OWN = 4
ORDER = (5, 3, 2, 0, 8, 6, 1, 7)
BANDS = XROWS // 16
TILE_BANDS = ROWS // 16


def dot(a, b):
    return jnp.dot(a, b, preferred_element_type=F32)


def dot_nt(a, b):
    return lax.dot_general(a, b, (((1,), (1,)), ((), ())), preferred_element_type=F32)


def iota(shape, dim):
    return lax.broadcasted_iota(I32, shape, dim)


def onehot(mask):
    return jnp.where(mask, 1.0, 0.0).astype(BF16)


def shifted_rows(row, rows, shift):
    wide = jnp.broadcast_to(row, (rows, row.shape[1]))
    return pltpu.roll(wide, shift, 1, stride=1, stride_axis=0)


def lanes(a, b):
    return jnp.concatenate([a, b], axis=1)


def kernel(
    nx, ny,
    taps_ref, owner_ref, offset_ref, est_hbm, tiles_hbm,
    out_ref,
    est_v, tiles_v, packed, arrived, ext, blurred, recip, quot, back_rows,
    center, side_out, side_in, row_out, row_in,
    kpad, row_fwd, row_bwd, col_fwd, col_bwd, depth_fwd, depth_bwd,
    index_v, index_s, slot_v, slot_s, label_out, label_in,
    load_sem, index_sem, store_sem,
    halo_send, halo_recv, tile_send, tile_recv, label_send, label_recv,
    side_send, side_recv, row_send, row_recv,
):
    gx, gy = lax.axis_index("gx"), lax.axis_index("gy")

    def device(dx, dy):
        return (lax.rem(gx + dx + nx, nx), lax.rem(gy + dy + ny, ny))

    def step_of(group):
        return group // 3 - 1, group % 3 - 1

    load_est = pltpu.make_async_copy(est_hbm, est_v, load_sem.at[0])
    load_tiles = pltpu.make_async_copy(tiles_hbm, tiles_v, load_sem.at[1])
    load_est.start()
    load_tiles.start()

    barrier = pltpu.get_barrier_semaphore()
    for group in ORDER:
        pl.semaphore_signal(barrier, inc=1, device_id=device(*step_of(group)), device_id_type=MESH)

    load_est.wait()
    zero_row = jnp.zeros((XCOLS, DEPTH), BF16)
    ext[0] = zero_row
    ext[XROWS - 1] = zero_row
    ext[HALO:HALO + ROWS, HALO:HALO + COLS, :] = est_v[...].astype(BF16)
    pl.semaphore_wait(barrier, len(ORDER))

    def send_halo(group, src, dst):
        copy = pltpu.make_async_remote_copy(
            src_ref=ext.at[src],
            dst_ref=ext.at[dst],
            send_sem=halo_send.at[group],
            recv_sem=halo_recv.at[group],
            device_id=device(*step_of(group)),
            device_id_type=MESH,
        )
        copy.start()
        return copy

    inner = slice(HALO, HALO + ROWS)
    halo_copies = [
        send_halo(5, (inner, slice(COLS, COLS + HALO)), (inner, slice(0, HALO))),
        send_halo(3, (inner, slice(HALO, 2 * HALO)), (inner, slice(HALO + COLS, XCOLS))),
    ]

    owner = owner_ref[...].reshape(1, TILES)
    shift = ny.bit_length() - 1

    def wrapped(d, n):
        return jnp.where(d == 0, 1, jnp.where(d == 1, 2, jnp.where(d == 1 - n, 2, 0)))

    group_of = wrapped((owner >> shift) - gx, nx) * 3 + wrapped((owner & (ny - 1)) - gy, ny)
    members = jnp.where(iota((16, TILES), 0) == group_of, 1.0, 0.0)
    before = onehot(iota((TILES, TILES), 0) < iota((TILES, TILES), 1))
    rank = jnp.sum(members * dot(members.astype(BF16), before), axis=0, keepdims=True)
    place = group_of * 128 + rank.astype(I32)
    picks = onehot(iota((9 * 128, TILES), 0) == place)
    number = iota((8, TILES), 1)
    row = iota((8, TILES), 0)
    offset = jnp.broadcast_to(offset_ref[...].reshape(1, TILES), (8, TILES))
    digits = jnp.where(row == 0, number >> 4, jnp.where(row == 1, number & 15, jnp.where(
        row == 2, offset >> 4, jnp.where(row == 3, offset & 15, 1))))
    found = dot_nt(digits.astype(F32).astype(BF16), picks)
    source = jnp.clip((found[0:1] * 16.0 + found[1:2]).astype(I32), 0, TILES - 1)
    label = (found[2:3] * 16.0 + found[3:4] + (found[4:5] - 1.0) * 1024.0).astype(I32)
    index_v[...] = jnp.zeros_like(index_v)
    for group in range(9):
        index_v[group:group + 1, :] = source[:, group * 128:(group + 1) * 128]
        label_out[group] = jnp.broadcast_to(label[:, group * 128:(group + 1) * 128], (8, 128))
    load_index = pltpu.make_async_copy(index_v, index_s, index_sem.at[0])
    load_index.start()
    label_copies = []
    for group in ORDER:
        copy = pltpu.make_async_remote_copy(
            src_ref=label_out.at[group],
            dst_ref=label_in.at[group],
            send_sem=label_send.at[group],
            recv_sem=label_recv.at[group],
            device_id=device(*step_of(group)),
            device_id_type=MESH,
        )
        copy.start()
        label_copies.append(copy)
    label_in[OWN] = label_out[OWN]

    load_index.wait()
    load_tiles.wait()
    tile_copies = []
    for group in ORDER:
        def pack(r, carry, group=group):
            packed[group * SLOTS + r] = tiles_v[index_s[group, r]]
            return carry

        lax.fori_loop(0, SLOTS, pack, 0, unroll=8)
        copy = pltpu.make_async_remote_copy(
            src_ref=packed.at[group * SLOTS:(group + 1) * SLOTS],
            dst_ref=arrived.at[group * SLOTS:(group + 1) * SLOTS],
            send_sem=tile_send.at[group],
            recv_sem=tile_recv.at[group],
            device_id=device(*step_of(group)),
            device_id_type=MESH,
        )
        copy.start()
        tile_copies.append(copy)

    def keep(r, carry):
        arrived[OWN * SLOTS + r] = tiles_v[index_s[OWN, r]]
        return carry

    lax.fori_loop(0, SLOTS, keep, 0, unroll=8)

    def clear(edge, rows, cols):
        @pl.when(edge)
        def _():
            ext[rows, cols, :] = jnp.zeros((rows.stop - rows.start, cols.stop - cols.start, DEPTH), BF16)

    for copy in halo_copies:
        copy.wait_recv()
    clear(gy == 0, inner, slice(0, HALO))
    clear(gy == ny - 1, inner, slice(HALO + COLS, XCOLS))
    row_halos = [
        send_halo(7, slice(ROWS + 1, ROWS + HALO), slice(1, HALO)),
        send_halo(1, slice(HALO, 2 * HALO - 1), slice(HALO + ROWS, XROWS - 1)),
    ]

    kpad[...] = jnp.zeros_like(kpad)
    kpad[:, 0:3, 0:TAPS] = taps_ref[...]
    spread = onehot((iota((256, 16), 0) >> 4) == iota((256, 16), 1))
    spread_wide = onehot((iota((768, 128), 0) >> 4) == iota((768, 128), 1))
    same = (iota((256, 256), 0) & 15) == (iota((256, 256), 1) & 15)
    eye = onehot(iota((128, 128), 0) == iota((128, 128), 1))
    depth_fwd[...] = jnp.zeros_like(depth_fwd)
    depth_bwd[...] = jnp.zeros_like(depth_bwd)
    for v in range(VIEWS):
        raw = kpad[v][0:3]
        norm = raw / jnp.sum(raw, axis=1, keepdims=True)
        rows_band = shifted_rows(norm[0:1], 16, 1).astype(BF16)
        wide = dot(spread, rows_band).astype(BF16)
        for d in range(3):
            fwd = dot_nt(wide, spread_wide[256 * d:256 * (d + 1)])
            row_fwd[v, :, 256 * d:256 * (d + 1)] = jnp.where(same, fwd, 0.0).astype(BF16)
            tall = dot_nt(spread_wide[256 * d:256 * (d + 1)], rows_band).astype(BF16)
            bwd = dot_nt(tall, spread)
            row_bwd[v, :, 256 * (2 - d):256 * (3 - d)] = jnp.where(same, bwd, 0.0).astype(BF16)
        cols_band = shifted_rows(norm[1:2], COLS, 1)
        col_fwd[v * COLS:(v + 1) * COLS, :] = cols_band.astype(BF16)
        long = lanes(norm[2:3], jnp.zeros((1, 128), F32))
        depth_t = shifted_rows(long, DEPTH, 128 - TAPS // 2)[:, 128:256].astype(BF16)
        at = slice(128 * (v % 2), 128 * (v % 2) + 128)
        depth_bwd[v // 2, at, at] = depth_t
        depth_fwd[v // 2, at, at] = dot_nt(eye, depth_t).astype(BF16)
    col_bwd[...] = dot_nt(eye[0:XCOLS], col_fwd[...]).astype(BF16)

    for copy in row_halos:
        copy.wait_recv()
    halo_copies += row_halos
    clear(gx == 0, slice(0, HALO), slice(0, XCOLS))
    clear(gx == nx - 1, slice(XROWS - HALO, XROWS), slice(0, XCOLS))

    def columns(p, carry):
        a = 2 * p
        both = lanes(ext[a], ext[a + 1])
        out = dot(col_fwd[:, 0:XCOLS], both).astype(BF16)
        blurred[a] = out[:, 0:128].reshape(VIEWS, COLS, DEPTH)
        blurred[a + 1] = out[:, 128:256].reshape(VIEWS, COLS, DEPTH)
        return carry

    lax.fori_loop(0, XROWS // 2, columns, 0, unroll=8)

    def rows_depth(n, carry):
        band, pair = n // 3, n % 3
        first = pl.multiple_of(band * 16, 16)
        parts = []
        for e in range(2):
            block = blurred[pl.ds(first, 48), 2 * pair + e]
            both = lanes(block[:, 0:16].reshape(768, DEPTH), block[:, 16:32].reshape(768, DEPTH))
            parts.append(dot(row_fwd[2 * pair + e], both).astype(BF16))
        for h in range(2):
            both = lanes(parts[0][:, 128 * h:128 * h + 128], parts[1][:, 128 * h:128 * h + 128])
            inverse = 1.0 / dot(both, depth_fwd[pair])
            for e in range(2):
                recip[2 * pair + e, pl.ds(first, 16), 16 * h:16 * h + 16, :] = inverse[
                    :, 128 * e:128 * e + 128].reshape(16, 16, DEPTH)
        return carry

    lax.fori_loop(0, TILE_BANDS * 3, rows_depth, 0, unroll=3)

    for copy in label_copies:
        copy.wait_recv()
    labels = jnp.concatenate([label_in[group][0:1] for group in range(9)], axis=1)
    where_is = onehot(iota((TILES, 9 * 128), 0) == labels)
    place_no = iota((8, 9 * 128), 1)
    place_digits = jnp.where(iota((8, 9 * 128), 0) == 0, place_no >> 7, place_no & 127)
    got = dot_nt(place_digits.astype(F32).astype(BF16), where_is)
    slots = jnp.clip((got[0:1] * float(SLOTS) + got[1:2]).astype(I32), 0, 9 * SLOTS - 1)
    slot_v[...] = jnp.zeros_like(slot_v)
    for n in range(3):
        slot_v[n:n + 1, :] = slots[:, 128 * n:128 * (n + 1)]
    load_slots = pltpu.make_async_copy(slot_v, slot_s, index_sem.at[1])
    load_slots.start()
    load_slots.wait()
    for copy in tile_copies:
        copy.wait_recv()

    side_copies, row_copies = [], []
    for band in range(BANDS):
        if band < TILE_BANDS:
            def quotients(pair, carry, band=band):
                tiles = []
                for i in range(16):
                    halves = []
                    for e in range(2):
                        at = slot_s[pair, 64 * e + 16 * band + i]
                        value = arrived[at].astype(F32) * recip[2 * pair + e, 16 * band + i]
                        halves.append(value.astype(BF16))
                    tiles.append(lanes(halves[0], halves[1]))
                out = dot(jnp.concatenate(tiles, axis=0), depth_bwd[pair]).astype(BF16)
                for e in range(2):
                    quot[2 * pair + e, 16 * band:16 * band + 16] = out[
                        :, 128 * e:128 * e + 128].reshape(16, COLS, DEPTH)
                return carry

            lax.fori_loop(0, 3, quotients, 0, unroll=3)
        s0, s1 = max(0, band - 2), min(TILE_BANDS - 1, band)
        w0, w1 = 256 * (2 - (band - s0)), 256 * (3 - (band - s1))

        def rows_back(v, carry, s0=s0, s1=s1, w0=w0, w1=w1):
            block = quot[v, 16 * s0:16 * (s1 + 1)]
            both = lanes(block[:, 0:16].reshape(w1 - w0, DEPTH), block[:, 16:32].reshape(w1 - w0, DEPTH))
            out = dot(row_bwd[v, :, w0:w1], both).astype(BF16)
            back_rows[:, v, 0:16, :] = out[:, 0:128].reshape(16, 16, DEPTH)
            back_rows[:, v, 16:32, :] = out[:, 128:256].reshape(16, 16, DEPTH)
            return carry

        lax.fori_loop(0, VIEWS, rows_back, 0, unroll=6)

        def cols_back(p, carry, band=band):
            both = lanes(back_rows[2 * p].reshape(VIEWS * COLS, DEPTH), back_rows[2 * p + 1].reshape(VIEWS * COLS, DEPTH))
            out = dot(col_bwd[...], both)
            for e in range(2):
                one = out[:, 128 * e:128 * e + 128]
                side_out[band, 0, 2 * p + e] = one[0:HALO].astype(BF16)
                side_out[band, 1, 2 * p + e] = one[HALO + COLS:XCOLS].astype(BF16)
                mid = one[HALO:HALO + COLS]
                if 1 <= band <= TILE_BANDS:
                    center[16 * (band - 1) + 2 * p + e] = mid
                else:
                    row_out[band // (BANDS - 1), 2 * p + e] = mid.astype(BF16)
            return carry

        lax.fori_loop(0, 8, cols_back, 0, unroll=8)
        dx = -1 if band == 0 else 1 if band == BANDS - 1 else 0
        for side in range(2):
            copy = pltpu.make_async_remote_copy(
                src_ref=side_out.at[band, side],
                dst_ref=side_in.at[band, side],
                send_sem=side_send.at[band, side],
                recv_sem=side_recv.at[band, side],
                device_id=device(dx, 2 * side - 1),
                device_id_type=MESH,
            )
            copy.start()
            side_copies.append(copy)
        if dx != 0:
            end = band // (BANDS - 1)
            copy = pltpu.make_async_remote_copy(
                src_ref=row_out.at[end],
                dst_ref=row_in.at[end],
                send_sem=row_send.at[end],
                recv_sem=row_recv.at[end],
                device_id=device(dx, 0),
                device_id_type=MESH,
            )
            copy.start()
            row_copies.append(copy)

    from_right, from_left = gy != ny - 1, gy != 0

    def sides(band, inside):
        for copy in side_copies[2 * band:2 * band + 2]:
            copy.wait_recv()
        low = side_in[band, 1].astype(F32)
        high = side_in[band, 0].astype(F32)
        return jnp.concatenate([
            jnp.where(jnp.logical_and(from_left, inside), low, 0.0),
            jnp.where(jnp.logical_and(from_right, inside), high, 0.0),
        ], axis=1)

    stores = []
    for c in (1, 2, 0, 3):
        rows = slice(16 * c, 16 * c + 16)
        total = center[rows] + sides(c + 1, True)
        if c == 0:
            inside = gx != 0
            row_copies[1].wait_recv()
            total = total + sides(BANDS - 1, inside) + jnp.where(inside, row_in[1].astype(F32), 0.0)
        if c == TILE_BANDS - 1:
            inside = gx != nx - 1
            row_copies[0].wait_recv()
            total = total + sides(0, inside) + jnp.where(inside, row_in[0].astype(F32), 0.0)
        center[rows] = est_v[rows] * (total * (1.0 / VIEWS))
        store = pltpu.make_async_copy(center.at[rows], out_ref.at[rows], store_sem.at[c])
        store.start()
        stores.append(store)

    for store in stores:
        store.wait()
    for copy in halo_copies + label_copies + tile_copies + side_copies + row_copies:
        copy.wait_send()


def body(view_tiles, tile_owner, tile_offset, estimate, spread_taps):
    nx, ny = lax.axis_size("gx"), lax.axis_size("gy")
    vmem = pl.BlockSpec(memory_space=pltpu.VMEM)
    anywhere = pl.BlockSpec(memory_space=pl.ANY)
    dma = pltpu.SemaphoreType.DMA
    return pl.pallas_call(
        lambda *refs: kernel(nx, ny, *refs),
        out_shape=jax.ShapeDtypeStruct((ROWS, COLS, DEPTH), F32),
        in_specs=[vmem, vmem, vmem, anywhere, anywhere],
        out_specs=anywhere,
        scratch_shapes=[
            pltpu.VMEM((ROWS, COLS, DEPTH), F32),
            pltpu.VMEM((TILES, COLS, DEPTH), BF16),
            pltpu.VMEM((9 * SLOTS, COLS, DEPTH), BF16),
            pltpu.VMEM((9 * SLOTS, COLS, DEPTH), BF16),
            pltpu.VMEM((XROWS, XCOLS, DEPTH), BF16),
            pltpu.VMEM((XROWS, VIEWS, COLS, DEPTH), BF16),
            pltpu.VMEM((VIEWS, ROWS, COLS, DEPTH), F32),
            pltpu.VMEM((VIEWS, ROWS, COLS, DEPTH), BF16),
            pltpu.VMEM((16, VIEWS, COLS, DEPTH), BF16),
            pltpu.VMEM((ROWS, COLS, DEPTH), F32),
            pltpu.VMEM((BANDS, 2, 16, HALO, DEPTH), BF16),
            pltpu.VMEM((BANDS, 2, 16, HALO, DEPTH), BF16),
            pltpu.VMEM((2, 16, COLS, DEPTH), BF16),
            pltpu.VMEM((2, 16, COLS, DEPTH), BF16),
            pltpu.VMEM((VIEWS, 8, 128), F32),
            pltpu.VMEM((VIEWS, 256, 768), BF16),
            pltpu.VMEM((VIEWS, 256, 768), BF16),
            pltpu.VMEM((VIEWS * COLS, 128), BF16),
            pltpu.VMEM((XCOLS, VIEWS * COLS), BF16),
            pltpu.VMEM((VIEWS // 2, 256, 256), BF16),
            pltpu.VMEM((VIEWS // 2, 256, 256), BF16),
            pltpu.VMEM((16, 128), I32),
            pltpu.SMEM((16, 128), I32),
            pltpu.VMEM((8, 128), I32),
            pltpu.SMEM((8, 128), I32),
            pltpu.VMEM((9, 8, 128), I32),
            pltpu.VMEM((9, 8, 128), I32),
            dma((2,)), dma((2,)), dma((4,)),
            dma((9,)), dma((9,)), dma((9,)), dma((9,)), dma((9,)), dma((9,)),
            dma((BANDS, 2)), dma((BANDS, 2)), dma((2,)), dma((2,)),
        ],
        compiler_params=pltpu.CompilerParams(
            collective_id=0, has_side_effects=True, vmem_limit_bytes=56 * 1024 * 1024
        ),
        name="richardson_lucy",
    )(spread_taps, tile_owner, tile_offset, estimate, view_tiles)


def solution(mesh):
    placed = (
        P(("gx", "gy"), None, None),
        P(("gx", "gy")),
        P(("gx", "gy")),
        P("gx", "gy", None),
        P(),
    )
    return jax.shard_map(
        body, mesh=mesh, in_specs=placed, out_specs=P("gx", "gy", None), check_vma=False
    )
```

```python
import jax
import jax.numpy as jnp
from jax import lax
from jax.experimental import pallas as pl
from jax.experimental.pallas import tpu as pltpu
from jax.sharding import PartitionSpec as P

MESH = pl.DeviceIdType.MESH
F32, BF16, I32 = jnp.float32, jnp.bfloat16, jnp.int32

VIEWS, TAPS = 6, 31
ROWS, COLS, DEPTH = 64, 32, 128
TILES = 384
HALO = 16
XROWS, XCOLS = ROWS + 2 * HALO, COLS + 2 * HALO
SLOTS = 64
OWN = 4
ORDER = (5, 3, 2, 0, 8, 6, 1, 7)
BANDS = XROWS // 16
TILE_BANDS = ROWS // 16


def dot(a, b):
    return jnp.dot(a, b, preferred_element_type=F32)


def dot_nt(a, b):
    return lax.dot_general(a, b, (((1,), (1,)), ((), ())), preferred_element_type=F32)


def iota(shape, dim):
    return lax.broadcasted_iota(I32, shape, dim)


def onehot(mask):
    return jnp.where(mask, 1.0, 0.0).astype(BF16)


def shifted_rows(row, rows, shift):
    wide = jnp.broadcast_to(row, (rows, row.shape[1]))
    return pltpu.roll(wide, shift, 1, stride=1, stride_axis=0)


def guarded(condition, action):
    if condition is None:
        action()
    else:
        pl.when(condition)(action)


class Send:
    def __init__(self, src, dst, send_sem, recv_sem, target, sends=None, receives=None):
        self.copy = pltpu.make_async_remote_copy(
            src_ref=src, dst_ref=dst, send_sem=send_sem, recv_sem=recv_sem,
            device_id=target, device_id_type=MESH,
        )
        self.sends, self.receives = sends, receives
        guarded(sends, self.copy.start)

    def wait_recv(self):
        guarded(self.receives, self.copy.wait_recv)

    def wait_send(self):
        guarded(self.sends, self.copy.wait_send)


def lanes(a, b):
    return jnp.concatenate([a, b], axis=1)


def kernel(
    nx, ny,
    taps_hbm, owner_hbm, offset_hbm, est_hbm, tiles_hbm,
    out_ref,
    est_v, tiles_v, packed, arrived, ext, blurred, recip, quot, back_rows,
    center, side_out, side_in, row_out, row_in,
    taps_ref, owner_ref, offset_ref, kpad, row_fwd, row_bwd, col_fwd, col_bwd, depth_fwd, depth_bwd,
    index_v, index_s, slot_v, slot_s, label_out, label_in,
    load_sem, index_sem, relay,
    halo_send, halo_recv, tile_send, tile_recv, label_send, label_recv,
    side_send, side_recv, row_send, row_recv,
):
    gx, gy = lax.axis_index("gx"), lax.axis_index("gy")

    def device(dx, dy):
        return (lax.rem(gx + dx + nx, nx), lax.rem(gy + dy + ny, ny))

    def step_of(group):
        return group // 3 - 1, group % 3 - 1

    barrier = pltpu.get_barrier_semaphore()
    for group in (5, 3, 1, 7):
        pl.semaphore_signal(barrier, inc=1, device_id=device(*step_of(group)), device_id_type=MESH)

    load_est = pltpu.make_async_copy(est_hbm, est_v, load_sem.at[0])
    load_owner = pltpu.make_async_copy(owner_hbm, owner_ref, load_sem.at[2])
    load_offset = pltpu.make_async_copy(offset_hbm, offset_ref, load_sem.at[3])
    load_tiles = pltpu.make_async_copy(tiles_hbm, tiles_v, load_sem.at[1])
    load_taps = pltpu.make_async_copy(taps_hbm, taps_ref, load_sem.at[4])
    load_est.start()
    load_owner.start()
    load_offset.start()
    load_tiles.start()
    load_taps.start()

    load_est.wait()
    zero_row = jnp.zeros((XCOLS, DEPTH), BF16)
    ext[0] = zero_row
    ext[XROWS - 1] = zero_row
    ext[HALO:HALO + ROWS, HALO:HALO + COLS, :] = est_v[...].astype(BF16)
    pl.semaphore_wait(barrier, 4)

    up, down, right, left = gx != nx - 1, gx != 0, gy != ny - 1, gy != 0

    def send_halo(group, src, dst, sends, receives):
        return Send(
            ext.at[src], ext.at[dst], halo_send.at[group], halo_recv.at[group],
            device(*step_of(group)), sends, receives,
        )

    inner = slice(HALO, HALO + ROWS)
    halo_copies = [
        send_halo(5, (inner, slice(COLS, COLS + HALO)), (inner, slice(0, HALO)), right, left),
        send_halo(3, (inner, slice(HALO, 2 * HALO)), (inner, slice(HALO + COLS, XCOLS)), left, right),
    ]

    for group in (5, 3):
        pl.semaphore_signal(relay, inc=1, device_id=device(*step_of(group)), device_id_type=MESH)

    load_owner.wait()
    load_offset.wait()
    owner = owner_ref[...].reshape(1, TILES)
    shift = ny.bit_length() - 1

    def wrapped(d, n):
        return jnp.where(d == 0, 1, jnp.where(d == 1, 2, jnp.where(d == 1 - n, 2, 0)))

    group_of = wrapped((owner >> shift) - gx, nx) * 3 + wrapped((owner & (ny - 1)) - gy, ny)
    members = jnp.where(iota((16, TILES), 0) == group_of, 1.0, 0.0)
    before = onehot(iota((TILES, TILES), 0) < iota((TILES, TILES), 1))
    rank = jnp.sum(members * dot(members.astype(BF16), before), axis=0, keepdims=True)
    place = group_of * 128 + rank.astype(I32)
    picks = onehot(iota((9 * 128, TILES), 0) == place)
    number = iota((8, TILES), 1)
    row = iota((8, TILES), 0)
    offset = jnp.broadcast_to(offset_ref[...].reshape(1, TILES), (8, TILES))
    digits = jnp.where(row == 0, number >> 4, jnp.where(row == 1, number & 15, jnp.where(
        row == 2, offset >> 4, jnp.where(row == 3, offset & 15, 1))))
    found = dot_nt(digits.astype(F32).astype(BF16), picks)
    source = jnp.clip((found[0:1] * 16.0 + found[1:2]).astype(I32), 0, TILES - 1)
    label = (found[2:3] * 16.0 + found[3:4] + (found[4:5] - 1.0) * 1024.0).astype(I32)
    index_v[...] = jnp.zeros_like(index_v)
    for group in range(9):
        index_v[group:group + 1, :] = source[:, group * 128:(group + 1) * 128]
        label_out[group] = jnp.broadcast_to(label[:, group * 128:(group + 1) * 128], (8, 128))
    load_index = pltpu.make_async_copy(index_v, index_s, index_sem.at[0])
    load_index.start()
    label_in[OWN] = label_out[OWN]

    load_index.wait()
    load_tiles.wait()
    label_copies, tile_copies = [], []
    for group in ORDER:
        def pack(r, carry, group=group):
            packed[group * SLOTS + r] = tiles_v[index_s[group, r]]
            return carry

        lax.fori_loop(0, SLOTS, pack, 0, unroll=8)
        if group == ORDER[2]:
            pl.semaphore_wait(relay, 2)
            label_copies = [
                Send(
                    label_out.at[other], label_in.at[other], label_send.at[other], label_recv.at[other],
                    device(*step_of(other)),
                )
                for other in ORDER
            ]
        slots = slice(group * SLOTS, (group + 1) * SLOTS)
        tile_copies.append(Send(
            packed.at[slots], arrived.at[slots], tile_send.at[group], tile_recv.at[group],
            device(*step_of(group)),
        ))

    def keep(r, carry):
        arrived[OWN * SLOTS + r] = tiles_v[index_s[OWN, r]]
        return carry

    lax.fori_loop(0, SLOTS, keep, 0, unroll=8)

    def clear(edge, rows, cols):
        @pl.when(edge)
        def _():
            ext[rows, cols, :] = jnp.zeros((rows.stop - rows.start, cols.stop - cols.start, DEPTH), BF16)

    for copy in halo_copies:
        copy.wait_recv()
    clear(gy == 0, inner, slice(0, HALO))
    clear(gy == ny - 1, inner, slice(HALO + COLS, XCOLS))
    row_halos = [
        send_halo(7, slice(ROWS + 1, ROWS + HALO), slice(1, HALO), up, down),
        send_halo(1, slice(HALO, 2 * HALO - 1), slice(HALO + ROWS, XROWS - 1), down, up),
    ]

    load_taps.wait()
    kpad[...] = jnp.zeros_like(kpad)
    kpad[:, 0:3, 0:TAPS] = taps_ref[...]
    spread = onehot((iota((256, 16), 0) >> 4) == iota((256, 16), 1))
    spread_wide = onehot((iota((768, 128), 0) >> 4) == iota((768, 128), 1))
    same = (iota((256, 256), 0) & 15) == (iota((256, 256), 1) & 15)
    eye = onehot(iota((128, 128), 0) == iota((128, 128), 1))
    depth_fwd[...] = jnp.zeros_like(depth_fwd)
    depth_bwd[...] = jnp.zeros_like(depth_bwd)
    for v in range(VIEWS):
        raw = kpad[v][0:3]
        norm = raw / jnp.sum(raw, axis=1, keepdims=True)
        rows_band = shifted_rows(norm[0:1], 16, 1).astype(BF16)
        wide = dot(spread, rows_band).astype(BF16)
        for d in range(3):
            fwd = dot_nt(wide, spread_wide[256 * d:256 * (d + 1)])
            row_fwd[v, :, 256 * d:256 * (d + 1)] = jnp.where(same, fwd, 0.0).astype(BF16)
            tall = dot_nt(spread_wide[256 * d:256 * (d + 1)], rows_band).astype(BF16)
            bwd = dot_nt(tall, spread)
            row_bwd[v, :, 256 * (2 - d):256 * (3 - d)] = jnp.where(same, bwd, 0.0).astype(BF16)
        cols_band = shifted_rows(norm[1:2], COLS, 1)
        col_fwd[v * COLS:(v + 1) * COLS, :] = cols_band.astype(BF16)
        long = lanes(norm[2:3], jnp.zeros((1, 128), F32))
        depth_t = shifted_rows(long, DEPTH, 128 - TAPS // 2)[:, 128:256].astype(BF16)
        at = slice(128 * (v % 2), 128 * (v % 2) + 128)
        depth_bwd[v // 2, at, at] = depth_t
        depth_fwd[v // 2, at, at] = dot_nt(eye, depth_t).astype(BF16)
    col_bwd[...] = dot_nt(eye[0:XCOLS], col_fwd[...]).astype(BF16)

    for copy in row_halos:
        copy.wait_recv()
    halo_copies += row_halos
    clear(gx == 0, slice(0, HALO), slice(0, XCOLS))
    clear(gx == nx - 1, slice(XROWS - HALO, XROWS), slice(0, XCOLS))

    def columns(p, carry):
        a = 2 * p
        both = lanes(ext[a], ext[a + 1])
        out = dot(col_fwd[:, 0:XCOLS], both).astype(BF16)
        blurred[a] = out[:, 0:128].reshape(VIEWS, COLS, DEPTH)
        blurred[a + 1] = out[:, 128:256].reshape(VIEWS, COLS, DEPTH)
        return carry

    lax.fori_loop(0, XROWS // 2, columns, 0, unroll=8)

    def rows_depth(n, carry):
        band, pair = n // 3, n % 3
        first = pl.multiple_of(band * 16, 16)
        parts = []
        for e in range(2):
            block = blurred[pl.ds(first, 48), 2 * pair + e]
            both = lanes(block[:, 0:16].reshape(768, DEPTH), block[:, 16:32].reshape(768, DEPTH))
            parts.append(dot(row_fwd[2 * pair + e], both).astype(BF16))
        for h in range(2):
            both = lanes(parts[0][:, 128 * h:128 * h + 128], parts[1][:, 128 * h:128 * h + 128])
            inverse = 1.0 / dot(both, depth_fwd[pair])
            for e in range(2):
                recip[2 * pair + e, pl.ds(first, 16), 16 * h:16 * h + 16, :] = inverse[
                    :, 128 * e:128 * e + 128].reshape(16, 16, DEPTH)
        return carry

    lax.fori_loop(0, TILE_BANDS * 3, rows_depth, 0, unroll=3)

    for copy in label_copies:
        copy.wait_recv()
    labels = jnp.concatenate([label_in[group][0:1] for group in range(9)], axis=1)
    where_is = onehot(iota((TILES, 9 * 128), 0) == labels)
    place_no = iota((8, 9 * 128), 1)
    place_digits = jnp.where(iota((8, 9 * 128), 0) == 0, place_no >> 7, place_no & 127)
    got = dot_nt(place_digits.astype(F32).astype(BF16), where_is)
    slots = jnp.clip((got[0:1] * float(SLOTS) + got[1:2]).astype(I32), 0, 9 * SLOTS - 1)
    slot_v[...] = jnp.zeros_like(slot_v)
    for n in range(3):
        slot_v[n:n + 1, :] = slots[:, 128 * n:128 * (n + 1)]
    load_slots = pltpu.make_async_copy(slot_v, slot_s, index_sem.at[1])
    load_slots.start()
    load_slots.wait()
    for copy in tile_copies:
        copy.wait_recv()

    side_copies, row_copies = [], []
    for band in range(BANDS):
        if band < TILE_BANDS:
            def quotients(pair, carry, band=band):
                tiles = []
                for i in range(16):
                    halves = []
                    for e in range(2):
                        at = slot_s[pair, 64 * e + 16 * band + i]
                        value = arrived[at].astype(F32) * recip[2 * pair + e, 16 * band + i]
                        halves.append(value.astype(BF16))
                    tiles.append(lanes(halves[0], halves[1]))
                out = dot(jnp.concatenate(tiles, axis=0), depth_bwd[pair]).astype(BF16)
                for e in range(2):
                    quot[2 * pair + e, 16 * band:16 * band + 16] = out[
                        :, 128 * e:128 * e + 128].reshape(16, COLS, DEPTH)
                return carry

            lax.fori_loop(0, 3, quotients, 0, unroll=3)
        s0, s1 = max(0, band - 2), min(TILE_BANDS - 1, band)
        w0, w1 = 256 * (2 - (band - s0)), 256 * (3 - (band - s1))

        def rows_back(v, carry, s0=s0, s1=s1, w0=w0, w1=w1):
            block = quot[v, 16 * s0:16 * (s1 + 1)]
            both = lanes(block[:, 0:16].reshape(w1 - w0, DEPTH), block[:, 16:32].reshape(w1 - w0, DEPTH))
            out = dot(row_bwd[v, :, w0:w1], both).astype(BF16)
            back_rows[:, v, 0:16, :] = out[:, 0:128].reshape(16, 16, DEPTH)
            back_rows[:, v, 16:32, :] = out[:, 128:256].reshape(16, 16, DEPTH)
            return carry

        lax.fori_loop(0, VIEWS, rows_back, 0, unroll=6)

        def cols_back(p, carry, band=band):
            both = lanes(back_rows[2 * p].reshape(VIEWS * COLS, DEPTH), back_rows[2 * p + 1].reshape(VIEWS * COLS, DEPTH))
            out = dot(col_bwd[...], both)
            for e in range(2):
                one = out[:, 128 * e:128 * e + 128]
                side_out[band, 0, 2 * p + e] = one[0:HALO].astype(BF16)
                side_out[band, 1, 2 * p + e] = one[HALO + COLS:XCOLS].astype(BF16)
                mid = one[HALO:HALO + COLS]
                if 1 <= band <= TILE_BANDS:
                    center[16 * (band - 1) + 2 * p + e] = mid
                else:
                    row_out[band // (BANDS - 1), 2 * p + e] = mid.astype(BF16)
            return carry

        lax.fori_loop(0, 8, cols_back, 0, unroll=8)
        dx = -1 if band == 0 else 1 if band == BANDS - 1 else 0
        sends, receives = {0: (None, None), -1: (down, up), 1: (up, down)}[dx]
        for side in range(2):
            out_of, into = (left, right) if side == 0 else (right, left)
            if dx != 0:
                out_of, into = jnp.logical_and(out_of, sends), jnp.logical_and(into, receives)
            side_copies.append(Send(
                side_out.at[band, side], side_in.at[band, side],
                side_send.at[band, side], side_recv.at[band, side],
                device(dx, 2 * side - 1), out_of, into,
            ))
        if dx != 0:
            end = band // (BANDS - 1)
            row_copies.append(Send(
                row_out.at[end], row_in.at[end], row_send.at[end], row_recv.at[end],
                device(dx, 0), sends, receives,
            ))

    def sides(band, inside):
        for copy in side_copies[2 * band:2 * band + 2]:
            copy.wait_recv()
        low = side_in[band, 1].astype(F32)
        high = side_in[band, 0].astype(F32)
        return jnp.concatenate([
            jnp.where(jnp.logical_and(left, inside), low, 0.0),
            jnp.where(jnp.logical_and(right, inside), high, 0.0),
        ], axis=1)

    for c in (1, 2, 0, 3):
        rows = slice(16 * c, 16 * c + 16)
        total = center[rows] + sides(c + 1, True)
        if c == 0:
            row_copies[1].wait_recv()
            total = total + sides(BANDS - 1, down) + jnp.where(down, row_in[1].astype(F32), 0.0)
        if c == TILE_BANDS - 1:
            row_copies[0].wait_recv()
            total = total + sides(0, up) + jnp.where(up, row_in[0].astype(F32), 0.0)
        out_ref[rows] = est_v[rows] * (total * (1.0 / VIEWS))

    for copy in halo_copies + label_copies + tile_copies + side_copies + row_copies:
        copy.wait_send()


def body(view_tiles, tile_owner, tile_offset, estimate, spread_taps):
    nx, ny = lax.axis_size("gx"), lax.axis_size("gy")
    vmem = pl.BlockSpec(memory_space=pltpu.VMEM)
    anywhere = pl.BlockSpec(memory_space=pl.ANY)
    dma = pltpu.SemaphoreType.DMA
    return pl.pallas_call(
        lambda *refs: kernel(nx, ny, *refs),
        out_shape=pltpu.VMEM((ROWS, COLS, DEPTH), F32),
        in_specs=[anywhere] * 5,
        out_specs=vmem,
        scratch_shapes=[
            pltpu.VMEM((ROWS, COLS, DEPTH), F32),
            pltpu.VMEM((TILES, COLS, DEPTH), BF16),
            pltpu.VMEM((9 * SLOTS, COLS, DEPTH), BF16),
            pltpu.VMEM((9 * SLOTS, COLS, DEPTH), BF16),
            pltpu.VMEM((XROWS, XCOLS, DEPTH), BF16),
            pltpu.VMEM((XROWS, VIEWS, COLS, DEPTH), BF16),
            pltpu.VMEM((VIEWS, ROWS, COLS, DEPTH), F32),
            pltpu.VMEM((VIEWS, ROWS, COLS, DEPTH), BF16),
            pltpu.VMEM((16, VIEWS, COLS, DEPTH), BF16),
            pltpu.VMEM((ROWS, COLS, DEPTH), F32),
            pltpu.VMEM((BANDS, 2, 16, HALO, DEPTH), BF16),
            pltpu.VMEM((BANDS, 2, 16, HALO, DEPTH), BF16),
            pltpu.VMEM((2, 16, COLS, DEPTH), BF16),
            pltpu.VMEM((2, 16, COLS, DEPTH), BF16),
            pltpu.VMEM((VIEWS, 3, TAPS), F32),
            pltpu.VMEM((TILES,), I32),
            pltpu.VMEM((TILES,), I32),
            pltpu.VMEM((VIEWS, 8, 128), F32),
            pltpu.VMEM((VIEWS, 256, 768), BF16),
            pltpu.VMEM((VIEWS, 256, 768), BF16),
            pltpu.VMEM((VIEWS * COLS, 128), BF16),
            pltpu.VMEM((XCOLS, VIEWS * COLS), BF16),
            pltpu.VMEM((VIEWS // 2, 256, 256), BF16),
            pltpu.VMEM((VIEWS // 2, 256, 256), BF16),
            pltpu.VMEM((16, 128), I32),
            pltpu.SMEM((16, 128), I32),
            pltpu.VMEM((8, 128), I32),
            pltpu.SMEM((8, 128), I32),
            pltpu.VMEM((9, 8, 128), I32),
            pltpu.VMEM((9, 8, 128), I32),
            dma((5,)), dma((2,)), pltpu.SemaphoreType.REGULAR,
            dma((9,)), dma((9,)), dma((9,)), dma((9,)), dma((9,)), dma((9,)),
            dma((BANDS, 2)), dma((BANDS, 2)), dma((2,)), dma((2,)),
        ],
        compiler_params=pltpu.CompilerParams(
            collective_id=0, has_side_effects=True, vmem_limit_bytes=56 * 1024 * 1024
        ),
        name="richardson_lucy",
    )(spread_taps, tile_owner, tile_offset, estimate, view_tiles)


def solution(mesh):
    placed = (
        P(("gx", "gy"), None, None),
        P(("gx", "gy")),
        P(("gx", "gy")),
        P("gx", "gy", None),
        P(),
    )
    return jax.shard_map(
        body, mesh=mesh, in_specs=placed, out_specs=P("gx", "gy", None), check_vma=False
    )
```

```python
import jax
import jax.numpy as jnp
from jax import lax
from jax.experimental import pallas as pl
from jax.experimental.pallas import tpu as pltpu
from jax.sharding import PartitionSpec as P

MESH = pl.DeviceIdType.MESH
F32, BF16, I32 = jnp.float32, jnp.bfloat16, jnp.int32

VIEWS, TAPS = 6, 31
ROWS, COLS, DEPTH = 64, 32, 128
TILES = 384
HALO = 16
XROWS, XCOLS = ROWS + 2 * HALO, COLS + 2 * HALO
SLOTS = 64
WIDE = 640
OWN = 4
ORDER = (8, 6, 2, 0, 7, 1, 5, 3)
BANDS = XROWS // 16
TILE_BANDS = ROWS // 16


def dot(a, b):
    return jnp.dot(a, b, preferred_element_type=F32)


def dot_nt(a, b):
    return lax.dot_general(a, b, (((1,), (1,)), ((), ())), preferred_element_type=F32)


def iota(shape, dim):
    return lax.broadcasted_iota(I32, shape, dim)


def onehot(mask):
    return jnp.where(mask, 1.0, 0.0).astype(BF16)


def shifted_rows(row, rows, shift):
    wide = jnp.broadcast_to(row, (rows, row.shape[1]))
    return pltpu.roll(wide, shift, 1, stride=1, stride_axis=0)


def guarded(condition, action):
    if condition is None:
        action()
    else:
        pl.when(condition)(action)


class Send:
    def __init__(self, src, dst, send_sem, recv_sem, target, sends=None, receives=None):
        self.copy = pltpu.make_async_remote_copy(
            src_ref=src, dst_ref=dst, send_sem=send_sem, recv_sem=recv_sem,
            device_id=target, device_id_type=MESH,
        )
        self.sends, self.receives = sends, receives
        guarded(sends, self.copy.start)

    def wait_recv(self):
        guarded(self.receives, self.copy.wait_recv)

    def wait_send(self):
        guarded(self.sends, self.copy.wait_send)


def lanes(a, b):
    return jnp.concatenate([a, b], axis=1)


def kernel(
    nx, ny,
    taps_hbm, owner_hbm, offset_hbm, est_hbm, tiles_hbm,
    out_ref,
    est_v, tiles_v, packed, arrived, ext, blurred, recip, quot, back_rows,
    center, side_out, side_in, row_out, row_in,
    taps_ref, owner_ref, offset_ref, kpad, row_fwd, row_bwd, col_fwd, col_bwd, depth_fwd, depth_bwd,
    index_v, index_s, slot_v, slot_s, label_out, label_in,
    load_sem, index_sem, relay,
    halo_send, halo_recv, tile_send, tile_recv, label_send, label_recv,
    side_send, side_recv, row_send, row_recv,
):
    gx, gy = lax.axis_index("gx"), lax.axis_index("gy")

    def device(dx, dy):
        return (lax.rem(gx + dx + nx, nx), lax.rem(gy + dy + ny, ny))

    def step_of(group):
        return group // 3 - 1, group % 3 - 1

    barrier = pltpu.get_barrier_semaphore()
    for group in (5, 3, 1, 7):
        pl.semaphore_signal(barrier, inc=1, device_id=device(*step_of(group)), device_id_type=MESH)

    load_est = pltpu.make_async_copy(est_hbm, est_v, load_sem.at[0])
    load_owner = pltpu.make_async_copy(owner_hbm, owner_ref, load_sem.at[2])
    load_offset = pltpu.make_async_copy(offset_hbm, offset_ref, load_sem.at[3])
    load_tiles = pltpu.make_async_copy(tiles_hbm, tiles_v, load_sem.at[1])
    load_taps = pltpu.make_async_copy(taps_hbm, taps_ref, load_sem.at[4])
    load_est.start()
    load_owner.start()
    load_offset.start()
    load_tiles.start()
    load_taps.start()

    load_owner.wait()
    load_offset.wait()
    owner = owner_ref[...].reshape(1, TILES)
    shift = ny.bit_length() - 1

    def wrapped(d, n):
        return jnp.where(d == 0, 1, jnp.where(d == 1, 2, jnp.where(d == 1 - n, 2, 0)))

    group_of = wrapped((owner >> shift) - gx, nx) * 3 + wrapped((owner & (ny - 1)) - gy, ny)
    members = jnp.where(iota((16, TILES), 0) == group_of, 1.0, 0.0)
    before = onehot(iota((TILES, TILES), 0) < iota((TILES, TILES), 1))
    rank = jnp.sum(members * dot(members.astype(BF16), before), axis=0, keepdims=True)
    place = group_of * SLOTS + rank.astype(I32)
    picks = onehot(iota((WIDE, TILES), 0) == place)
    number = iota((8, TILES), 1)
    row = iota((8, TILES), 0)
    offset = jnp.broadcast_to(offset_ref[...].reshape(1, TILES), (8, TILES))
    digits = jnp.where(row == 0, number >> 4, jnp.where(row == 1, number & 15, jnp.where(
        row == 2, offset >> 4, jnp.where(row == 3, offset & 15, 1))))
    found = dot_nt(digits.astype(F32).astype(BF16), picks)
    source = jnp.clip((found[0:1] * 16.0 + found[1:2]).astype(I32), 0, TILES - 1)
    label = (found[2:3] * 16.0 + found[3:4] + (found[4:5] - 1.0) * 1024.0).astype(I32)
    index_v[...] = jnp.zeros_like(index_v)
    for n in range(WIDE // 128):
        index_v[n:n + 1, :] = source[:, n * 128:(n + 1) * 128]
        for group in range(2 * n, min(2 * n + 2, 9)):
            label_out[group] = jnp.broadcast_to(label[:, n * 128:(n + 1) * 128], (8, 128))
    load_index = pltpu.make_async_copy(index_v, index_s, index_sem.at[0])
    load_index.start()

    load_est.wait()
    zero_row = jnp.zeros((XCOLS, DEPTH), BF16)
    ext[0] = zero_row
    ext[XROWS - 1] = zero_row
    ext[HALO:HALO + ROWS, HALO:HALO + COLS, :] = est_v[...].astype(BF16)
    pl.semaphore_wait(barrier, 4)

    up, down, right, left = gx != nx - 1, gx != 0, gy != ny - 1, gy != 0

    def send_halo(group, src, dst, sends, receives):
        return Send(
            ext.at[src], ext.at[dst], halo_send.at[group], halo_recv.at[group],
            device(*step_of(group)), sends, receives,
        )

    inner = slice(HALO, HALO + ROWS)
    halo_copies = [
        send_halo(5, (inner, slice(COLS, COLS + HALO)), (inner, slice(0, HALO)), right, left),
        send_halo(3, (inner, slice(HALO, 2 * HALO)), (inner, slice(HALO + COLS, XCOLS)), left, right),
    ]

    for group in (5, 3):
        pl.semaphore_signal(relay, inc=1, device_id=device(*step_of(group)), device_id_type=MESH)

    label_in[OWN] = label_out[OWN]

    load_index.wait()
    load_tiles.wait()
    label_copies, tile_copies = [], []
    for group in ORDER:
        def pack(r, carry, group=group):
            packed[group * SLOTS + r] = tiles_v[index_s[group // 2, group % 2 * SLOTS + r]]
            return carry

        lax.fori_loop(0, SLOTS, pack, 0, unroll=8)
        if group == ORDER[0]:
            pl.semaphore_wait(relay, 2)
            label_copies = [
                Send(
                    label_out.at[other], label_in.at[other], label_send.at[other], label_recv.at[other],
                    device(*step_of(other)),
                )
                for other in ORDER
            ]
        slots = slice(group * SLOTS, (group + 1) * SLOTS)
        tile_copies.append(Send(
            packed.at[slots], arrived.at[slots], tile_send.at[group], tile_recv.at[group],
            device(*step_of(group)),
        ))

    def keep(r, carry):
        arrived[OWN * SLOTS + r] = tiles_v[index_s[OWN // 2, OWN % 2 * SLOTS + r]]
        return carry

    lax.fori_loop(0, SLOTS, keep, 0, unroll=8)

    def clear(edge, rows, cols):
        @pl.when(edge)
        def _():
            ext[rows, cols, :] = jnp.zeros((rows.stop - rows.start, cols.stop - cols.start, DEPTH), BF16)

    for copy in halo_copies:
        copy.wait_recv()
    clear(gy == 0, inner, slice(0, HALO))
    clear(gy == ny - 1, inner, slice(HALO + COLS, XCOLS))
    row_halos = [
        send_halo(7, slice(ROWS + 1, ROWS + HALO), slice(1, HALO), up, down),
        send_halo(1, slice(HALO, 2 * HALO - 1), slice(HALO + ROWS, XROWS - 1), down, up),
    ]

    load_taps.wait()
    kpad[...] = jnp.zeros_like(kpad)
    kpad[:, 0:3, 0:TAPS] = taps_ref[...]
    spread = onehot((iota((256, 16), 0) >> 4) == iota((256, 16), 1))
    spread_wide = onehot((iota((768, 128), 0) >> 4) == iota((768, 128), 1))
    same = (iota((256, 256), 0) & 15) == (iota((256, 256), 1) & 15)
    eye = onehot(iota((128, 128), 0) == iota((128, 128), 1))
    depth_fwd[...] = jnp.zeros_like(depth_fwd)
    depth_bwd[...] = jnp.zeros_like(depth_bwd)
    for v in range(VIEWS):
        raw = kpad[v][0:3]
        norm = raw / jnp.sum(raw, axis=1, keepdims=True)
        rows_band = shifted_rows(norm[0:1], 16, 1).astype(BF16)
        wide = dot(spread, rows_band).astype(BF16)
        for d in range(3):
            fwd = dot_nt(wide, spread_wide[256 * d:256 * (d + 1)])
            row_fwd[v, :, 256 * d:256 * (d + 1)] = jnp.where(same, fwd, 0.0).astype(BF16)
            tall = dot_nt(spread_wide[256 * d:256 * (d + 1)], rows_band).astype(BF16)
            bwd = dot_nt(tall, spread)
            row_bwd[v, :, 256 * (2 - d):256 * (3 - d)] = jnp.where(same, bwd, 0.0).astype(BF16)
        cols_band = shifted_rows(norm[1:2], COLS, 1)
        col_fwd[v * COLS:(v + 1) * COLS, :] = cols_band.astype(BF16)
        long = lanes(norm[2:3], jnp.zeros((1, 128), F32))
        depth_t = shifted_rows(long, DEPTH, 128 - TAPS // 2)[:, 128:256].astype(BF16)
        at = slice(128 * (v % 2), 128 * (v % 2) + 128)
        depth_bwd[v // 2, at, at] = depth_t
        depth_fwd[v // 2, at, at] = dot_nt(eye, depth_t).astype(BF16)
    col_bwd[...] = dot_nt(eye[0:XCOLS], col_fwd[...]).astype(BF16)

    for copy in row_halos:
        copy.wait_recv()
    halo_copies += row_halos
    clear(gx == 0, slice(0, HALO), slice(0, XCOLS))
    clear(gx == nx - 1, slice(XROWS - HALO, XROWS), slice(0, XCOLS))

    def columns(p, carry):
        a = 2 * p
        both = lanes(ext[a], ext[a + 1])
        out = dot(col_fwd[:, 0:XCOLS], both).astype(BF16)
        blurred[a] = out[:, 0:128].reshape(VIEWS, COLS, DEPTH)
        blurred[a + 1] = out[:, 128:256].reshape(VIEWS, COLS, DEPTH)
        return carry

    lax.fori_loop(0, XROWS // 2, columns, 0, unroll=8)

    def rows_depth(n, carry):
        band, pair = n // 3, n % 3
        first = pl.multiple_of(band * 16, 16)
        parts = []
        for e in range(2):
            block = blurred[pl.ds(first, 48), 2 * pair + e]
            both = lanes(block[:, 0:16].reshape(768, DEPTH), block[:, 16:32].reshape(768, DEPTH))
            parts.append(dot(row_fwd[2 * pair + e], both).astype(BF16))
        for h in range(2):
            both = lanes(parts[0][:, 128 * h:128 * h + 128], parts[1][:, 128 * h:128 * h + 128])
            inverse = 1.0 / dot(both, depth_fwd[pair])
            for e in range(2):
                recip[2 * pair + e, pl.ds(first, 16), 16 * h:16 * h + 16, :] = inverse[
                    :, 128 * e:128 * e + 128].reshape(16, 16, DEPTH)
        return carry

    lax.fori_loop(0, TILE_BANDS * 3, rows_depth, 0, unroll=3)

    for copy in label_copies:
        copy.wait_recv()
    first_half = iota((1, 128), 1) < SLOTS
    nobody = jnp.full((1, 128), -1, I32)
    labels = jnp.concatenate([
        jnp.where(first_half, label_in[2 * n][0:1], label_in[2 * n + 1][0:1] if 2 * n + 1 < 9 else nobody)
        for n in range(WIDE // 128)
    ], axis=1)
    where_is = onehot(iota((TILES, WIDE), 0) == labels)
    slot_no = iota((8, WIDE), 1)
    slot_digits = jnp.where(iota((8, WIDE), 0) == 0, slot_no >> 4, slot_no & 15)
    got = dot_nt(slot_digits.astype(F32).astype(BF16), where_is)
    slots = jnp.clip((got[0:1] * 16.0 + got[1:2]).astype(I32), 0, 9 * SLOTS - 1)
    slot_v[...] = jnp.zeros_like(slot_v)
    for n in range(3):
        slot_v[n:n + 1, :] = slots[:, 128 * n:128 * (n + 1)]
    load_slots = pltpu.make_async_copy(slot_v, slot_s, index_sem.at[1])
    load_slots.start()
    load_slots.wait()
    for copy in tile_copies:
        copy.wait_recv()

    side_copies, row_copies = [], []
    for band in range(BANDS):
        if band < TILE_BANDS:
            def quotients(pair, carry, band=band):
                tiles = []
                for i in range(16):
                    halves = []
                    for e in range(2):
                        at = slot_s[pair, 64 * e + 16 * band + i]
                        value = arrived[at].astype(F32) * recip[2 * pair + e, 16 * band + i]
                        halves.append(value.astype(BF16))
                    tiles.append(lanes(halves[0], halves[1]))
                out = dot(jnp.concatenate(tiles, axis=0), depth_bwd[pair]).astype(BF16)
                for e in range(2):
                    quot[2 * pair + e, 16 * band:16 * band + 16] = out[
                        :, 128 * e:128 * e + 128].reshape(16, COLS, DEPTH)
                return carry

            lax.fori_loop(0, 3, quotients, 0, unroll=3)
        s0, s1 = max(0, band - 2), min(TILE_BANDS - 1, band)
        w0, w1 = 256 * (2 - (band - s0)), 256 * (3 - (band - s1))

        def rows_back(v, carry, s0=s0, s1=s1, w0=w0, w1=w1):
            block = quot[v, 16 * s0:16 * (s1 + 1)]
            both = lanes(block[:, 0:16].reshape(w1 - w0, DEPTH), block[:, 16:32].reshape(w1 - w0, DEPTH))
            out = dot(row_bwd[v, :, w0:w1], both).astype(BF16)
            back_rows[:, v, 0:16, :] = out[:, 0:128].reshape(16, 16, DEPTH)
            back_rows[:, v, 16:32, :] = out[:, 128:256].reshape(16, 16, DEPTH)
            return carry

        lax.fori_loop(0, VIEWS, rows_back, 0, unroll=6)

        def cols_back(p, carry, band=band):
            both = lanes(back_rows[2 * p].reshape(VIEWS * COLS, DEPTH), back_rows[2 * p + 1].reshape(VIEWS * COLS, DEPTH))
            out = dot(col_bwd[...], both)
            for e in range(2):
                one = out[:, 128 * e:128 * e + 128]
                side_out[band, 0, 2 * p + e] = one[0:HALO].astype(BF16)
                side_out[band, 1, 2 * p + e] = one[HALO + COLS:XCOLS].astype(BF16)
                mid = one[HALO:HALO + COLS]
                if 1 <= band <= TILE_BANDS:
                    center[16 * (band - 1) + 2 * p + e] = mid
                else:
                    row_out[band // (BANDS - 1), 2 * p + e] = mid.astype(BF16)
            return carry

        lax.fori_loop(0, 8, cols_back, 0, unroll=8)
        dx = -1 if band == 0 else 1 if band == BANDS - 1 else 0
        sends, receives = {0: (None, None), -1: (down, up), 1: (up, down)}[dx]
        for side in range(2):
            out_of, into = (left, right) if side == 0 else (right, left)
            if dx != 0:
                out_of, into = jnp.logical_and(out_of, sends), jnp.logical_and(into, receives)
            side_copies.append(Send(
                side_out.at[band, side], side_in.at[band, side],
                side_send.at[band, side], side_recv.at[band, side],
                device(dx, 2 * side - 1), out_of, into,
            ))
        if dx != 0:
            end = band // (BANDS - 1)
            row_copies.append(Send(
                row_out.at[end], row_in.at[end], row_send.at[end], row_recv.at[end],
                device(dx, 0), sends, receives,
            ))

    def sides(band, inside):
        for copy in side_copies[2 * band:2 * band + 2]:
            copy.wait_recv()
        low = side_in[band, 1].astype(F32)
        high = side_in[band, 0].astype(F32)
        return jnp.concatenate([
            jnp.where(jnp.logical_and(left, inside), low, 0.0),
            jnp.where(jnp.logical_and(right, inside), high, 0.0),
        ], axis=1)

    for c in (1, 2, 3, 0):
        rows = slice(16 * c, 16 * c + 16)
        total = center[rows] + sides(c + 1, True)
        if c == 0:
            row_copies[1].wait_recv()
            total = total + sides(BANDS - 1, down) + jnp.where(down, row_in[1].astype(F32), 0.0)
        if c == TILE_BANDS - 1:
            row_copies[0].wait_recv()
            total = total + sides(0, up) + jnp.where(up, row_in[0].astype(F32), 0.0)
        out_ref[rows] = est_v[rows] * (total * (1.0 / VIEWS))

    for copy in halo_copies + label_copies + tile_copies + side_copies + row_copies:
        copy.wait_send()


def body(view_tiles, tile_owner, tile_offset, estimate, spread_taps):
    nx, ny = lax.axis_size("gx"), lax.axis_size("gy")
    vmem = pl.BlockSpec(memory_space=pltpu.VMEM)
    anywhere = pl.BlockSpec(memory_space=pl.ANY)
    dma = pltpu.SemaphoreType.DMA
    return pl.pallas_call(
        lambda *refs: kernel(nx, ny, *refs),
        out_shape=pltpu.VMEM((ROWS, COLS, DEPTH), F32),
        in_specs=[anywhere] * 5,
        out_specs=vmem,
        scratch_shapes=[
            pltpu.VMEM((ROWS, COLS, DEPTH), F32),
            pltpu.VMEM((TILES, COLS, DEPTH), BF16),
            pltpu.VMEM((9 * SLOTS, COLS, DEPTH), BF16),
            pltpu.VMEM((9 * SLOTS, COLS, DEPTH), BF16),
            pltpu.VMEM((XROWS, XCOLS, DEPTH), BF16),
            pltpu.VMEM((XROWS, VIEWS, COLS, DEPTH), BF16),
            pltpu.VMEM((VIEWS, ROWS, COLS, DEPTH), F32),
            pltpu.VMEM((VIEWS, ROWS, COLS, DEPTH), BF16),
            pltpu.VMEM((16, VIEWS, COLS, DEPTH), BF16),
            pltpu.VMEM((ROWS, COLS, DEPTH), F32),
            pltpu.VMEM((BANDS, 2, 16, HALO, DEPTH), BF16),
            pltpu.VMEM((BANDS, 2, 16, HALO, DEPTH), BF16),
            pltpu.VMEM((2, 16, COLS, DEPTH), BF16),
            pltpu.VMEM((2, 16, COLS, DEPTH), BF16),
            pltpu.VMEM((VIEWS, 3, TAPS), F32),
            pltpu.VMEM((TILES,), I32),
            pltpu.VMEM((TILES,), I32),
            pltpu.VMEM((VIEWS, 8, 128), F32),
            pltpu.VMEM((VIEWS, 256, 768), BF16),
            pltpu.VMEM((VIEWS, 256, 768), BF16),
            pltpu.VMEM((VIEWS * COLS, 128), BF16),
            pltpu.VMEM((XCOLS, VIEWS * COLS), BF16),
            pltpu.VMEM((VIEWS // 2, 256, 256), BF16),
            pltpu.VMEM((VIEWS // 2, 256, 256), BF16),
            pltpu.VMEM((8, 128), I32),
            pltpu.SMEM((8, 128), I32),
            pltpu.VMEM((8, 128), I32),
            pltpu.SMEM((8, 128), I32),
            pltpu.VMEM((9, 8, 128), I32),
            pltpu.VMEM((9, 8, 128), I32),
            dma((5,)), dma((2,)), pltpu.SemaphoreType.REGULAR,
            dma((9,)), dma((9,)), dma((9,)), dma((9,)), dma((9,)), dma((9,)),
            dma((BANDS, 2)), dma((BANDS, 2)), dma((2,)), dma((2,)),
        ],
        compiler_params=pltpu.CompilerParams(
            collective_id=0, has_side_effects=True, vmem_limit_bytes=56 * 1024 * 1024
        ),
        name="richardson_lucy",
    )(spread_taps, tile_owner, tile_offset, estimate, view_tiles)


def solution(mesh):
    placed = (
        P(("gx", "gy"), None, None),
        P(("gx", "gy")),
        P(("gx", "gy")),
        P("gx", "gy", None),
        P(),
    )
    return jax.shard_map(
        body, mesh=mesh, in_specs=placed, out_specs=P("gx", "gy", None), check_vma=False
    )
```

```python
import jax
import jax.numpy as jnp
from jax import lax
from jax.experimental import pallas as pl
from jax.experimental.pallas import tpu as pltpu
from jax.sharding import PartitionSpec as P

MESH = pl.DeviceIdType.MESH
F32, BF16, I32 = jnp.float32, jnp.bfloat16, jnp.int32

VIEWS, TAPS = 6, 31
ROWS, COLS, DEPTH = 64, 32, 128
TILES = 384
HALO = 16
XROWS, XCOLS = ROWS + 2 * HALO, COLS + 2 * HALO
SLOTS = 64
WIDE = 640
OWN = 4
ORDER = (8, 6, 2, 0, 7, 1, 5, 3)
BANDS = XROWS // 16
TILE_BANDS = ROWS // 16


def dot(a, b):
    return jnp.dot(a, b, preferred_element_type=F32)


def dot_nt(a, b):
    return lax.dot_general(a, b, (((1,), (1,)), ((), ())), preferred_element_type=F32)


def iota(shape, dim):
    return lax.broadcasted_iota(I32, shape, dim)


def onehot(mask):
    return jnp.where(mask, 1.0, 0.0).astype(BF16)


def shifted_rows(row, rows, shift):
    wide = jnp.broadcast_to(row, (rows, row.shape[1]))
    return pltpu.roll(wide, shift, 1, stride=1, stride_axis=0)


def guarded(condition, action):
    if condition is None:
        action()
    else:
        pl.when(condition)(action)


class Send:
    def __init__(self, src, dst, send_sem, recv_sem, target, sends=None, receives=None):
        self.copy = pltpu.make_async_remote_copy(
            src_ref=src, dst_ref=dst, send_sem=send_sem, recv_sem=recv_sem,
            device_id=target, device_id_type=MESH,
        )
        self.sends, self.receives = sends, receives
        guarded(sends, self.copy.start)

    def wait_recv(self):
        guarded(self.receives, self.copy.wait_recv)

    def wait_send(self):
        guarded(self.sends, self.copy.wait_send)


def lanes(a, b):
    return jnp.concatenate([a, b], axis=1)


def kernel(
    nx, ny,
    taps_hbm, owner_hbm, offset_hbm, est_hbm, tiles_hbm,
    out_ref,
    est_v, tiles_v, packed, arrived, ext, blurred, recip, quot, back_rows,
    center, side_out, side_in, row_out, row_in,
    taps_ref, owner_ref, offset_ref, kpad, row_fwd, row_bwd, col_fwd, col_bwd, depth_fwd, depth_bwd,
    index_v, index_s, slot_v, slot_s, label_out, label_in,
    load_sem, index_sem, relay,
    halo_send, halo_recv, tile_send, tile_recv, label_send, label_recv,
    side_send, side_recv, row_send, row_recv,
):
    gx, gy = lax.axis_index("gx"), lax.axis_index("gy")

    def device(dx, dy):
        return (lax.rem(gx + dx + nx, nx), lax.rem(gy + dy + ny, ny))

    def step_of(group):
        return group // 3 - 1, group % 3 - 1

    barrier = pltpu.get_barrier_semaphore()
    for group in (5, 3, 1, 7):
        pl.semaphore_signal(barrier, inc=1, device_id=device(*step_of(group)), device_id_type=MESH)

    load_est = pltpu.make_async_copy(est_hbm, est_v, load_sem.at[0])
    load_owner = pltpu.make_async_copy(owner_hbm, owner_ref, load_sem.at[2])
    load_offset = pltpu.make_async_copy(offset_hbm, offset_ref, load_sem.at[3])
    load_tiles = pltpu.make_async_copy(tiles_hbm, tiles_v, load_sem.at[1])
    load_taps = pltpu.make_async_copy(taps_hbm, taps_ref, load_sem.at[4])
    load_est.start()
    load_owner.start()
    load_offset.start()
    load_tiles.start()
    load_taps.start()

    load_owner.wait()
    load_offset.wait()
    owner = owner_ref[...].reshape(1, TILES)
    shift = ny.bit_length() - 1

    def wrapped(d, n):
        return jnp.where(d == 0, 1, jnp.where(d == 1, 2, jnp.where(d == 1 - n, 2, 0)))

    group_of = wrapped((owner >> shift) - gx, nx) * 3 + wrapped((owner & (ny - 1)) - gy, ny)
    members = jnp.where(iota((16, TILES), 0) == group_of, 1.0, 0.0)
    before = onehot(iota((TILES, TILES), 0) < iota((TILES, TILES), 1))
    rank = jnp.sum(members * dot(members.astype(BF16), before), axis=0, keepdims=True)
    place = group_of * SLOTS + rank.astype(I32)
    picks = onehot(iota((WIDE, TILES), 0) == place)
    number = iota((8, TILES), 1)
    row = iota((8, TILES), 0)
    offset = jnp.broadcast_to(offset_ref[...].reshape(1, TILES), (8, TILES))
    digits = jnp.where(row == 0, number >> 4, jnp.where(row == 1, number & 15, jnp.where(
        row == 2, offset >> 4, jnp.where(row == 3, offset & 15, 1))))
    found = dot_nt(digits.astype(F32).astype(BF16), picks)
    source = jnp.clip((found[0:1] * 16.0 + found[1:2]).astype(I32), 0, TILES - 1)
    label = (found[2:3] * 16.0 + found[3:4] + (found[4:5] - 1.0) * 1024.0).astype(I32)
    index_v[...] = jnp.zeros_like(index_v)
    for n in range(WIDE // 128):
        index_v[n:n + 1, :] = source[:, n * 128:(n + 1) * 128]
        for group in range(2 * n, min(2 * n + 2, 9)):
            label_out[group] = jnp.broadcast_to(label[:, n * 128:(n + 1) * 128], (8, 128))
    load_index = pltpu.make_async_copy(index_v, index_s, index_sem.at[0])
    load_index.start()

    load_est.wait()
    zero_row = jnp.zeros((XCOLS, DEPTH), BF16)
    ext[0] = zero_row
    ext[XROWS - 1] = zero_row
    ext[HALO:HALO + ROWS, HALO:HALO + COLS, :] = est_v[...].astype(BF16)
    pl.semaphore_wait(barrier, 4)

    up, down, right, left = gx != nx - 1, gx != 0, gy != ny - 1, gy != 0

    def send_halo(group, src, dst, sends, receives):
        return Send(
            ext.at[src], ext.at[dst], halo_send.at[group], halo_recv.at[group],
            device(*step_of(group)), sends, receives,
        )

    inner = slice(HALO, HALO + ROWS)
    halo_copies = [
        send_halo(5, (inner, slice(COLS, COLS + HALO)), (inner, slice(0, HALO)), right, left),
        send_halo(3, (inner, slice(HALO, 2 * HALO)), (inner, slice(HALO + COLS, XCOLS)), left, right),
    ]

    for group in (5, 3):
        pl.semaphore_signal(relay, inc=1, device_id=device(*step_of(group)), device_id_type=MESH)

    label_in[OWN] = label_out[OWN]

    load_index.wait()
    load_tiles.wait()
    label_copies, tile_copies = [], []
    for group in ORDER:
        def pack(r, carry, group=group):
            packed[group * SLOTS + r] = tiles_v[index_s[group // 2, group % 2 * SLOTS + r]]
            return carry

        lax.fori_loop(0, SLOTS, pack, 0, unroll=8)
        if group == ORDER[0]:
            pl.semaphore_wait(relay, 2)
            label_copies = [
                Send(
                    label_out.at[other], label_in.at[other], label_send.at[other], label_recv.at[other],
                    device(*step_of(other)),
                )
                for other in ORDER
            ]
        slots = slice(group * SLOTS, (group + 1) * SLOTS)
        tile_copies.append(Send(
            packed.at[slots], arrived.at[slots], tile_send.at[group], tile_recv.at[group],
            device(*step_of(group)),
        ))

    def keep(r, carry):
        arrived[OWN * SLOTS + r] = tiles_v[index_s[OWN // 2, OWN % 2 * SLOTS + r]]
        return carry

    lax.fori_loop(0, SLOTS, keep, 0, unroll=8)

    def clear(edge, rows, cols):
        @pl.when(edge)
        def _():
            ext[rows, cols, :] = jnp.zeros((rows.stop - rows.start, cols.stop - cols.start, DEPTH), BF16)

    for copy in halo_copies:
        copy.wait_recv()
    clear(gy == 0, inner, slice(0, HALO))
    clear(gy == ny - 1, inner, slice(HALO + COLS, XCOLS))
    row_halos = [
        send_halo(7, slice(ROWS + 1, ROWS + HALO), slice(1, HALO), up, down),
        send_halo(1, slice(HALO, 2 * HALO - 1), slice(HALO + ROWS, XROWS - 1), down, up),
    ]

    load_taps.wait()
    kpad[...] = jnp.zeros_like(kpad)
    kpad[:, 0:3, 0:TAPS] = taps_ref[...]
    spread = onehot((iota((256, 16), 0) >> 4) == iota((256, 16), 1))
    spread_wide = onehot((iota((768, 128), 0) >> 4) == iota((768, 128), 1))
    same = (iota((256, 256), 0) & 15) == (iota((256, 256), 1) & 15)
    eye = onehot(iota((128, 128), 0) == iota((128, 128), 1))
    depth_fwd[...] = jnp.zeros_like(depth_fwd)
    depth_bwd[...] = jnp.zeros_like(depth_bwd)
    for v in range(VIEWS):
        raw = kpad[v][0:3]
        norm = raw / jnp.sum(raw, axis=1, keepdims=True)
        rows_band = shifted_rows(norm[0:1], 16, 1).astype(BF16)
        wide = dot(spread, rows_band).astype(BF16)
        for d in range(3):
            fwd = dot_nt(wide, spread_wide[256 * d:256 * (d + 1)])
            row_fwd[v, :, 256 * d:256 * (d + 1)] = jnp.where(same, fwd, 0.0).astype(BF16)
            tall = dot_nt(spread_wide[256 * d:256 * (d + 1)], rows_band).astype(BF16)
            bwd = dot_nt(tall, spread)
            row_bwd[v, :, 256 * (2 - d):256 * (3 - d)] = jnp.where(same, bwd, 0.0).astype(BF16)
        cols_band = shifted_rows(norm[1:2], COLS, 1)
        col_fwd[v * COLS:(v + 1) * COLS, :] = cols_band.astype(BF16)
        long = lanes(norm[2:3], jnp.zeros((1, 128), F32))
        depth_t = shifted_rows(long, DEPTH, 128 - TAPS // 2)[:, 128:256].astype(BF16)
        at = slice(128 * (v % 2), 128 * (v % 2) + 128)
        depth_bwd[v // 2, at, at] = depth_t
        depth_fwd[v // 2, at, at] = dot_nt(eye, depth_t).astype(BF16)
    col_bwd[...] = dot_nt(eye[0:XCOLS], col_fwd[...]).astype(BF16)

    for copy in row_halos:
        copy.wait_recv()
    halo_copies += row_halos
    clear(gx == 0, slice(0, HALO), slice(0, XCOLS))
    clear(gx == nx - 1, slice(XROWS - HALO, XROWS), slice(0, XCOLS))

    def columns(p, carry):
        a = 2 * p
        both = lanes(ext[a], ext[a + 1])
        out = dot(col_fwd[:, 0:XCOLS], both).astype(BF16)
        blurred[a] = out[:, 0:128].reshape(VIEWS, COLS, DEPTH)
        blurred[a + 1] = out[:, 128:256].reshape(VIEWS, COLS, DEPTH)
        return carry

    lax.fori_loop(0, XROWS // 2, columns, 0, unroll=8)

    def rows_depth(n, carry):
        band, pair = n // 3, n % 3
        first = pl.multiple_of(band * 16, 16)
        parts = []
        for e in range(2):
            block = blurred[pl.ds(first, 48), 2 * pair + e]
            both = lanes(block[:, 0:16].reshape(768, DEPTH), block[:, 16:32].reshape(768, DEPTH))
            parts.append(dot(row_fwd[2 * pair + e], both).astype(BF16))
        for h in range(2):
            both = lanes(parts[0][:, 128 * h:128 * h + 128], parts[1][:, 128 * h:128 * h + 128])
            inverse = 1.0 / dot(both, depth_fwd[pair])
            for e in range(2):
                recip[2 * pair + e, pl.ds(first, 16), 16 * h:16 * h + 16, :] = inverse[
                    :, 128 * e:128 * e + 128].reshape(16, 16, DEPTH)
        return carry

    lax.fori_loop(0, TILE_BANDS * 3, rows_depth, 0, unroll=3)

    for copy in label_copies:
        copy.wait_recv()
    first_half = iota((1, 128), 1) < SLOTS
    nobody = jnp.full((1, 128), -1, I32)
    labels = jnp.concatenate([
        jnp.where(first_half, label_in[2 * n][0:1], label_in[2 * n + 1][0:1] if 2 * n + 1 < 9 else nobody)
        for n in range(WIDE // 128)
    ], axis=1)
    where_is = onehot(iota((TILES, WIDE), 0) == labels)
    slot_no = iota((8, WIDE), 1)
    slot_digits = jnp.where(iota((8, WIDE), 0) == 0, slot_no >> 4, slot_no & 15)
    got = dot_nt(slot_digits.astype(F32).astype(BF16), where_is)
    slots = jnp.clip((got[0:1] * 16.0 + got[1:2]).astype(I32), 0, 9 * SLOTS - 1)
    slot_v[...] = jnp.zeros_like(slot_v)
    for n in range(3):
        slot_v[n:n + 1, :] = slots[:, 128 * n:128 * (n + 1)]
    load_slots = pltpu.make_async_copy(slot_v, slot_s, index_sem.at[1])
    load_slots.start()
    load_slots.wait()
    for copy in tile_copies:
        copy.wait_recv()

    def quotients_of(band):
        def quotients(pair, carry):
            tiles = []
            for i in range(16):
                halves = []
                for e in range(2):
                    at = slot_s[pair, 64 * e + 16 * band + i]
                    value = arrived[at].astype(F32) * recip[2 * pair + e, 16 * band + i]
                    halves.append(value.astype(BF16))
                tiles.append(lanes(halves[0], halves[1]))
            out = dot(jnp.concatenate(tiles, axis=0), depth_bwd[pair]).astype(BF16)
            for e in range(2):
                quot[2 * pair + e, 16 * band:16 * band + 16] = out[
                    :, 128 * e:128 * e + 128].reshape(16, COLS, DEPTH)
            return carry

        lax.fori_loop(0, 3, quotients, 0, unroll=3)

    def rows_of(band):
        s0, s1 = max(0, band - 2), min(TILE_BANDS - 1, band)
        w0, w1 = 256 * (2 - (band - s0)), 256 * (3 - (band - s1))
        buffer = band % 2

        def rows_back(v, carry):
            block = quot[v, 16 * s0:16 * (s1 + 1)]
            both = lanes(block[:, 0:16].reshape(w1 - w0, DEPTH), block[:, 16:32].reshape(w1 - w0, DEPTH))
            out = dot(row_bwd[v, :, w0:w1], both).astype(BF16)
            back_rows[buffer, :, v, 0:16, :] = out[:, 0:128].reshape(16, 16, DEPTH)
            back_rows[buffer, :, v, 16:32, :] = out[:, 128:256].reshape(16, 16, DEPTH)
            return carry

        lax.fori_loop(0, VIEWS, rows_back, 0, unroll=6)

    def cols_of(band):
        buffer = band % 2

        def cols_back(p, carry):
            both = lanes(
                back_rows[buffer, 2 * p].reshape(VIEWS * COLS, DEPTH),
                back_rows[buffer, 2 * p + 1].reshape(VIEWS * COLS, DEPTH),
            )
            out = dot(col_bwd[...], both)
            for e in range(2):
                one = out[:, 128 * e:128 * e + 128]
                side_out[band, 0, 2 * p + e] = one[0:HALO].astype(BF16)
                side_out[band, 1, 2 * p + e] = one[HALO + COLS:XCOLS].astype(BF16)
                mid = one[HALO:HALO + COLS]
                if 1 <= band <= TILE_BANDS:
                    center[16 * (band - 1) + 2 * p + e] = mid
                else:
                    row_out[band // (BANDS - 1), 2 * p + e] = mid.astype(BF16)
            return carry

        lax.fori_loop(0, 8, cols_back, 0, unroll=8)

    side_copies, row_copies = {}, {}

    def send_of(band):
        dx = -1 if band == 0 else 1 if band == BANDS - 1 else 0
        sends, receives = {0: (None, None), -1: (down, up), 1: (up, down)}[dx]
        side_copies[band] = []
        for side in range(2):
            out_of, into = (left, right) if side == 0 else (right, left)
            if dx != 0:
                out_of, into = jnp.logical_and(out_of, sends), jnp.logical_and(into, receives)
            side_copies[band].append(Send(
                side_out.at[band, side], side_in.at[band, side],
                side_send.at[band, side], side_recv.at[band, side],
                device(dx, 2 * side - 1), out_of, into,
            ))
        if dx != 0:
            end = band // (BANDS - 1)
            row_copies[end] = Send(
                row_out.at[end], row_in.at[end], row_send.at[end], row_recv.at[end],
                device(dx, 0), sends, receives,
            )

    quotients_of(0)
    rows_of(0)
    quotients_of(1)
    cols_of(0)
    send_of(0)
    rows_of(1)
    quotients_of(2)
    cols_of(1)
    send_of(1)
    rows_of(2)
    quotients_of(3)
    cols_of(2)
    send_of(2)
    rows_of(3)
    cols_of(3)
    send_of(3)
    rows_of(4)
    cols_of(4)
    send_of(4)
    rows_of(5)
    cols_of(5)
    send_of(5)
    for copy in halo_copies + label_copies + tile_copies:
        copy.wait_send()

    def sides(band, inside):
        for copy in side_copies[band]:
            copy.wait_recv()
        low = side_in[band, 1].astype(F32)
        high = side_in[band, 0].astype(F32)
        return jnp.concatenate([
            jnp.where(jnp.logical_and(left, inside), low, 0.0),
            jnp.where(jnp.logical_and(right, inside), high, 0.0),
        ], axis=1)

    for c in (1, 2, 3, 0):
        rows = slice(16 * c, 16 * c + 16)
        total = center[rows] + sides(c + 1, True)
        if c == 0:
            for copy in sum((side_copies[band] for band in range(BANDS - 1)), []):
                copy.wait_send()
            row_copies[1].wait_recv()
            total = total + sides(BANDS - 1, down) + jnp.where(down, row_in[1].astype(F32), 0.0)
        if c == TILE_BANDS - 1:
            row_copies[0].wait_recv()
            total = total + sides(0, up) + jnp.where(up, row_in[0].astype(F32), 0.0)
        out_ref[rows] = est_v[rows] * (total * (1.0 / VIEWS))

    for copy in side_copies[BANDS - 1] + list(row_copies.values()):
        copy.wait_send()


def body(view_tiles, tile_owner, tile_offset, estimate, spread_taps):
    nx, ny = lax.axis_size("gx"), lax.axis_size("gy")
    vmem = pl.BlockSpec(memory_space=pltpu.VMEM)
    anywhere = pl.BlockSpec(memory_space=pl.ANY)
    dma = pltpu.SemaphoreType.DMA
    return pl.pallas_call(
        lambda *refs: kernel(nx, ny, *refs),
        out_shape=pltpu.VMEM((ROWS, COLS, DEPTH), F32),
        in_specs=[anywhere] * 5,
        out_specs=vmem,
        scratch_shapes=[
            pltpu.VMEM((ROWS, COLS, DEPTH), F32),
            pltpu.VMEM((TILES, COLS, DEPTH), BF16),
            pltpu.VMEM((9 * SLOTS, COLS, DEPTH), BF16),
            pltpu.VMEM((9 * SLOTS, COLS, DEPTH), BF16),
            pltpu.VMEM((XROWS, XCOLS, DEPTH), BF16),
            pltpu.VMEM((XROWS, VIEWS, COLS, DEPTH), BF16),
            pltpu.VMEM((VIEWS, ROWS, COLS, DEPTH), F32),
            pltpu.VMEM((VIEWS, ROWS, COLS, DEPTH), BF16),
            pltpu.VMEM((2, 16, VIEWS, COLS, DEPTH), BF16),
            pltpu.VMEM((ROWS, COLS, DEPTH), F32),
            pltpu.VMEM((BANDS, 2, 16, HALO, DEPTH), BF16),
            pltpu.VMEM((BANDS, 2, 16, HALO, DEPTH), BF16),
            pltpu.VMEM((2, 16, COLS, DEPTH), BF16),
            pltpu.VMEM((2, 16, COLS, DEPTH), BF16),
            pltpu.VMEM((VIEWS, 3, TAPS), F32),
            pltpu.VMEM((TILES,), I32),
            pltpu.VMEM((TILES,), I32),
            pltpu.VMEM((VIEWS, 8, 128), F32),
            pltpu.VMEM((VIEWS, 256, 768), BF16),
            pltpu.VMEM((VIEWS, 256, 768), BF16),
            pltpu.VMEM((VIEWS * COLS, 128), BF16),
            pltpu.VMEM((XCOLS, VIEWS * COLS), BF16),
            pltpu.VMEM((VIEWS // 2, 256, 256), BF16),
            pltpu.VMEM((VIEWS // 2, 256, 256), BF16),
            pltpu.VMEM((8, 128), I32),
            pltpu.SMEM((8, 128), I32),
            pltpu.VMEM((8, 128), I32),
            pltpu.SMEM((8, 128), I32),
            pltpu.VMEM((9, 8, 128), I32),
            pltpu.VMEM((9, 8, 128), I32),
            dma((5,)), dma((2,)), pltpu.SemaphoreType.REGULAR,
            dma((9,)), dma((9,)), dma((9,)), dma((9,)), dma((9,)), dma((9,)),
            dma((BANDS, 2)), dma((BANDS, 2)), dma((2,)), dma((2,)),
        ],
        compiler_params=pltpu.CompilerParams(
            collective_id=0, has_side_effects=True, vmem_limit_bytes=56 * 1024 * 1024
        ),
        name="richardson_lucy",
    )(spread_taps, tile_owner, tile_offset, estimate, view_tiles)


def solution(mesh):
    placed = (
        P(("gx", "gy"), None, None),
        P(("gx", "gy")),
        P(("gx", "gy")),
        P("gx", "gy", None),
        P(),
    )
    return jax.shard_map(
        body, mesh=mesh, in_specs=placed, out_specs=P("gx", "gy", None), check_vma=False
    )
```

```python
import jax
import jax.numpy as jnp
from jax import lax
from jax.experimental import pallas as pl
from jax.experimental.pallas import tpu as pltpu
from jax.sharding import PartitionSpec as P

MESH = pl.DeviceIdType.MESH
F32, BF16, I32 = jnp.float32, jnp.bfloat16, jnp.int32

VIEWS, TAPS = 6, 31
ROWS, COLS, DEPTH = 64, 32, 128
TILES = 384
HALO = 16
XROWS, XCOLS = ROWS + 2 * HALO, COLS + 2 * HALO
SLOTS = 64
WIDE = 640
OWN = 4
ORDER = (8, 6, 2, 0, 7, 1, 5, 3)
BANDS = XROWS // 16
TILE_BANDS = ROWS // 16


def dot(a, b):
    return jnp.dot(a, b, preferred_element_type=F32)


def dot_nt(a, b):
    return lax.dot_general(a, b, (((1,), (1,)), ((), ())), preferred_element_type=F32)


def iota(shape, dim):
    return lax.broadcasted_iota(I32, shape, dim)


def onehot(mask):
    return jnp.where(mask, 1.0, 0.0).astype(BF16)


def shifted_rows(row, rows, shift):
    wide = jnp.broadcast_to(row, (rows, row.shape[1]))
    return pltpu.roll(wide, shift, 1, stride=1, stride_axis=0)


def guarded(condition, action):
    if condition is None:
        action()
    else:
        pl.when(condition)(action)


class Send:
    def __init__(self, src, dst, send_sem, recv_sem, target, sends=None, receives=None):
        self.copy = pltpu.make_async_remote_copy(
            src_ref=src, dst_ref=dst, send_sem=send_sem, recv_sem=recv_sem,
            device_id=target, device_id_type=MESH,
        )
        self.sends, self.receives = sends, receives
        guarded(sends, self.copy.start)

    def wait_recv(self):
        guarded(self.receives, self.copy.wait_recv)

    def wait_send(self):
        guarded(self.sends, self.copy.wait_send)


def lanes(a, b):
    return jnp.concatenate([a, b], axis=1)


def kernel(
    nx, ny,
    taps_hbm, owner_hbm, offset_hbm, est_hbm, tiles_hbm,
    out_ref,
    est_v, tiles_v, packed, arrived, ext, blurred, recip, quot, back_rows,
    center, side_out, side_in, row_out, row_in,
    taps_ref, owner_ref, offset_ref, kpad, row_fwd, row_bwd, col_fwd, col_bwd, depth_fwd, depth_bwd,
    index_v, index_s, slot_v, slot_s, label_out, label_in,
    load_sem, index_sem, relay,
    halo_send, halo_recv, tile_send, tile_recv, label_send, label_recv,
    side_send, side_recv, row_send, row_recv,
):
    gx, gy = lax.axis_index("gx"), lax.axis_index("gy")

    def device(dx, dy):
        return (lax.rem(gx + dx + nx, nx), lax.rem(gy + dy + ny, ny))

    def step_of(group):
        return group // 3 - 1, group % 3 - 1

    barrier = pltpu.get_barrier_semaphore()
    for group in (5, 3, 1, 7):
        pl.semaphore_signal(barrier, inc=1, device_id=device(*step_of(group)), device_id_type=MESH)

    load_est = pltpu.make_async_copy(est_hbm, est_v, load_sem.at[0])
    load_owner = pltpu.make_async_copy(owner_hbm, owner_ref, load_sem.at[2])
    load_offset = pltpu.make_async_copy(offset_hbm, offset_ref, load_sem.at[3])
    load_tiles = pltpu.make_async_copy(tiles_hbm, tiles_v, load_sem.at[1])
    load_taps = pltpu.make_async_copy(taps_hbm, taps_ref, load_sem.at[4])
    load_est.start()
    load_owner.start()
    load_offset.start()
    load_tiles.start()
    load_taps.start()

    load_owner.wait()
    load_offset.wait()
    owner = owner_ref[...].reshape(1, TILES)
    shift = ny.bit_length() - 1

    def wrapped(d, n):
        return jnp.where(d == 0, 1, jnp.where(d == 1, 2, jnp.where(d == 1 - n, 2, 0)))

    group_of = wrapped((owner >> shift) - gx, nx) * 3 + wrapped((owner & (ny - 1)) - gy, ny)
    members = jnp.where(iota((16, TILES), 0) == group_of, 1.0, 0.0)
    before = onehot(iota((TILES, TILES), 0) < iota((TILES, TILES), 1))
    rank = jnp.sum(members * dot(members.astype(BF16), before), axis=0, keepdims=True)
    place = group_of * SLOTS + rank.astype(I32)
    picks = onehot(iota((WIDE, TILES), 0) == place)
    number = iota((8, TILES), 1)
    row = iota((8, TILES), 0)
    offset = jnp.broadcast_to(offset_ref[...].reshape(1, TILES), (8, TILES))
    digits = jnp.where(row == 0, number >> 4, jnp.where(row == 1, number & 15, jnp.where(
        row == 2, offset >> 4, jnp.where(row == 3, offset & 15, 1))))
    found = dot_nt(digits.astype(F32).astype(BF16), picks)
    source = jnp.clip((found[0:1] * 16.0 + found[1:2]).astype(I32), 0, TILES - 1)
    label = (found[2:3] * 16.0 + found[3:4] + (found[4:5] - 1.0) * 1024.0).astype(I32)
    index_v[...] = jnp.zeros_like(index_v)
    for n in range(WIDE // 128):
        index_v[n:n + 1, :] = source[:, n * 128:(n + 1) * 128]
        for group in range(2 * n, min(2 * n + 2, 9)):
            label_out[group] = jnp.broadcast_to(label[:, n * 128:(n + 1) * 128], (8, 128))
    load_index = pltpu.make_async_copy(index_v, index_s, index_sem.at[0])
    load_index.start()

    load_est.wait()
    zero_row = jnp.zeros((XCOLS, DEPTH), BF16)
    ext[0] = zero_row
    ext[XROWS - 1] = zero_row
    ext[HALO:HALO + ROWS, HALO:HALO + COLS, :] = est_v[...].astype(BF16)
    pl.semaphore_wait(barrier, 4)

    up, down, right, left = gx != nx - 1, gx != 0, gy != ny - 1, gy != 0

    def send_halo(group, src, dst, sends, receives):
        return Send(
            ext.at[src], ext.at[dst], halo_send.at[group], halo_recv.at[group],
            device(*step_of(group)), sends, receives,
        )

    inner = slice(HALO, HALO + ROWS)
    halo_copies = [
        send_halo(5, (inner, slice(COLS, COLS + HALO)), (inner, slice(0, HALO)), right, left),
        send_halo(3, (inner, slice(HALO, 2 * HALO)), (inner, slice(HALO + COLS, XCOLS)), left, right),
    ]

    for group in (5, 3):
        pl.semaphore_signal(relay, inc=1, device_id=device(*step_of(group)), device_id_type=MESH)

    label_in[OWN] = label_out[OWN]

    load_index.wait()
    load_tiles.wait()
    label_copies, tile_copies = [], []
    for group in ORDER:
        def pack(r, carry, group=group):
            packed[group * SLOTS + r] = tiles_v[index_s[group // 2, group % 2 * SLOTS + r]]
            return carry

        lax.fori_loop(0, SLOTS, pack, 0, unroll=8)
        if group == ORDER[0]:
            pl.semaphore_wait(relay, 2)
            label_copies = [
                Send(
                    label_out.at[other], label_in.at[other], label_send.at[other], label_recv.at[other],
                    device(*step_of(other)),
                )
                for other in ORDER
            ]
        slots = slice(group * SLOTS, (group + 1) * SLOTS)
        tile_copies.append(Send(
            packed.at[slots], arrived.at[slots], tile_send.at[group], tile_recv.at[group],
            device(*step_of(group)),
        ))

    def keep(r, carry):
        arrived[OWN * SLOTS + r] = tiles_v[index_s[OWN // 2, OWN % 2 * SLOTS + r]]
        return carry

    lax.fori_loop(0, SLOTS, keep, 0, unroll=8)

    def clear(edge, rows, cols):
        @pl.when(edge)
        def _():
            ext[rows, cols, :] = jnp.zeros((rows.stop - rows.start, cols.stop - cols.start, DEPTH), BF16)

    for copy in halo_copies:
        copy.wait_recv()
    clear(gy == 0, inner, slice(0, HALO))
    clear(gy == ny - 1, inner, slice(HALO + COLS, XCOLS))
    row_halos = [
        send_halo(7, slice(ROWS + 1, ROWS + HALO), slice(1, HALO), up, down),
        send_halo(1, slice(HALO, 2 * HALO - 1), slice(HALO + ROWS, XROWS - 1), down, up),
    ]

    load_taps.wait()
    kpad[...] = jnp.zeros_like(kpad)
    kpad[:, 0:3, 0:TAPS] = taps_ref[...]
    spread = onehot((iota((256, 16), 0) >> 4) == iota((256, 16), 1))
    spread_wide = onehot((iota((768, 128), 0) >> 4) == iota((768, 128), 1))
    same = (iota((256, 256), 0) & 15) == (iota((256, 256), 1) & 15)
    eye = onehot(iota((128, 128), 0) == iota((128, 128), 1))
    depth_fwd[...] = jnp.zeros_like(depth_fwd)
    depth_bwd[...] = jnp.zeros_like(depth_bwd)
    for v in range(VIEWS):
        raw = kpad[v][0:3]
        norm = raw / jnp.sum(raw, axis=1, keepdims=True)
        rows_band = shifted_rows(norm[0:1], 16, 1).astype(BF16)
        wide = dot(spread, rows_band).astype(BF16)
        for d in range(3):
            fwd = dot_nt(wide, spread_wide[256 * d:256 * (d + 1)])
            row_fwd[v, :, 256 * d:256 * (d + 1)] = jnp.where(same, fwd, 0.0).astype(BF16)
            tall = dot_nt(spread_wide[256 * d:256 * (d + 1)], rows_band).astype(BF16)
            bwd = dot_nt(tall, spread)
            row_bwd[v, :, 256 * (2 - d):256 * (3 - d)] = jnp.where(same, bwd, 0.0).astype(BF16)
        cols_band = shifted_rows(norm[1:2], COLS, 1)
        col_fwd[v * COLS:(v + 1) * COLS, :] = cols_band.astype(BF16)
        long = lanes(norm[2:3], jnp.zeros((1, 128), F32))
        depth_t = shifted_rows(long, DEPTH, 128 - TAPS // 2)[:, 128:256].astype(BF16)
        at = slice(128 * (v % 2), 128 * (v % 2) + 128)
        depth_bwd[v // 2, at, at] = depth_t
        depth_fwd[v // 2, at, at] = dot_nt(eye, depth_t).astype(BF16)
    col_bwd[...] = dot_nt(eye[0:XCOLS], col_fwd[...]).astype(BF16)

    for copy in row_halos:
        copy.wait_recv()
    halo_copies += row_halos
    clear(gx == 0, slice(0, HALO), slice(0, XCOLS))
    clear(gx == nx - 1, slice(XROWS - HALO, XROWS), slice(0, XCOLS))

    def columns(p, carry):
        a = 2 * p
        both = lanes(ext[a], ext[a + 1])
        out = dot(col_fwd[:, 0:XCOLS], both).astype(BF16)
        blurred[a] = out[:, 0:128].reshape(VIEWS, COLS, DEPTH)
        blurred[a + 1] = out[:, 128:256].reshape(VIEWS, COLS, DEPTH)
        return carry

    lax.fori_loop(0, XROWS // 2, columns, 0, unroll=8)

    def rows_depth(n, carry):
        band, pair = n // 3, n % 3
        first = pl.multiple_of(band * 16, 16)
        parts = []
        for e in range(2):
            block = blurred[pl.ds(first, 48), 2 * pair + e]
            both = lanes(block[:, 0:16].reshape(768, DEPTH), block[:, 16:32].reshape(768, DEPTH))
            parts.append(dot(row_fwd[2 * pair + e], both).astype(BF16))
        for h in range(2):
            both = lanes(parts[0][:, 128 * h:128 * h + 128], parts[1][:, 128 * h:128 * h + 128])
            inverse = 1.0 / dot(both, depth_fwd[pair])
            for e in range(2):
                recip[2 * pair + e, pl.ds(first, 16), 16 * h:16 * h + 16, :] = inverse[
                    :, 128 * e:128 * e + 128].reshape(16, 16, DEPTH)
        return carry

    lax.fori_loop(0, TILE_BANDS * 3, rows_depth, 0, unroll=3)

    for copy in label_copies:
        copy.wait_recv()
    first_half = iota((1, 128), 1) < SLOTS
    nobody = jnp.full((1, 128), -1, I32)
    labels = jnp.concatenate([
        jnp.where(first_half, label_in[2 * n][0:1], label_in[2 * n + 1][0:1] if 2 * n + 1 < 9 else nobody)
        for n in range(WIDE // 128)
    ], axis=1)
    where_is = onehot(iota((TILES, WIDE), 0) == labels)
    slot_no = iota((8, WIDE), 1)
    slot_digits = jnp.where(iota((8, WIDE), 0) == 0, slot_no >> 4, slot_no & 15)
    got = dot_nt(slot_digits.astype(F32).astype(BF16), where_is)
    slots = jnp.clip((got[0:1] * 16.0 + got[1:2]).astype(I32), 0, 9 * SLOTS - 1)
    slot_v[...] = jnp.zeros_like(slot_v)
    for n in range(3):
        slot_v[n:n + 1, :] = slots[:, 128 * n:128 * (n + 1)]
    load_slots = pltpu.make_async_copy(slot_v, slot_s, index_sem.at[1])
    load_slots.start()
    load_slots.wait()
    for copy in tile_copies:
        copy.wait_recv()

    def quotients_of(band):
        def quotients(pair, carry):
            tiles = []
            for i in range(16):
                halves = []
                for e in range(2):
                    at = slot_s[pair, 64 * e + 16 * band + i]
                    value = arrived[at].astype(F32) * recip[2 * pair + e, 16 * band + i]
                    halves.append(value.astype(BF16))
                tiles.append(lanes(halves[0], halves[1]))
            out = dot(jnp.concatenate(tiles, axis=0), depth_bwd[pair]).astype(BF16)
            for e in range(2):
                quot[2 * pair + e, 16 * band:16 * band + 16] = out[
                    :, 128 * e:128 * e + 128].reshape(16, COLS, DEPTH)
            return carry

        lax.fori_loop(0, 3, quotients, 0, unroll=3)

    def rows_of(band):
        s0, s1 = max(0, band - 2), min(TILE_BANDS - 1, band)
        w0, w1 = 256 * (2 - (band - s0)), 256 * (3 - (band - s1))
        buffer = band % 2

        def rows_back(v, carry):
            block = quot[v, 16 * s0:16 * (s1 + 1)]
            both = lanes(block[:, 0:16].reshape(w1 - w0, DEPTH), block[:, 16:32].reshape(w1 - w0, DEPTH))
            out = dot(row_bwd[v, :, w0:w1], both).astype(BF16)
            back_rows[buffer, :, v, 0:16, :] = out[:, 0:128].reshape(16, 16, DEPTH)
            back_rows[buffer, :, v, 16:32, :] = out[:, 128:256].reshape(16, 16, DEPTH)
            return carry

        lax.fori_loop(0, VIEWS, rows_back, 0, unroll=6)

    def cols_of(band):
        buffer = band % 2

        def cols_back(p, carry):
            both = lanes(
                back_rows[buffer, 2 * p].reshape(VIEWS * COLS, DEPTH),
                back_rows[buffer, 2 * p + 1].reshape(VIEWS * COLS, DEPTH),
            )
            out = dot(col_bwd[...], both)
            for e in range(2):
                one = out[:, 128 * e:128 * e + 128]
                side_out[band, 0, 2 * p + e] = one[0:HALO].astype(BF16)
                side_out[band, 1, 2 * p + e] = one[HALO + COLS:XCOLS].astype(BF16)
                mid = one[HALO:HALO + COLS]
                if 1 <= band <= TILE_BANDS:
                    center[16 * (band - 1) + 2 * p + e] = mid
                else:
                    row_out[band // (BANDS - 1), 2 * p + e] = mid.astype(BF16)
            return carry

        lax.fori_loop(0, 8, cols_back, 0, unroll=8)

    side_copies, row_copies = {}, {}

    def send_of(band):
        dx = -1 if band == 0 else 1 if band == BANDS - 1 else 0
        sends, receives = {0: (None, None), -1: (down, up), 1: (up, down)}[dx]
        side_copies[band] = []
        for side in range(2):
            out_of, into = (left, right) if side == 0 else (right, left)
            if dx != 0:
                out_of, into = jnp.logical_and(out_of, sends), jnp.logical_and(into, receives)
            side_copies[band].append(Send(
                side_out.at[band, side], side_in.at[band, side],
                side_send.at[band, side], side_recv.at[band, side],
                device(dx, 2 * side - 1), out_of, into,
            ))
        if dx != 0:
            end = band // (BANDS - 1)
            row_copies[end] = Send(
                row_out.at[end], row_in.at[end], row_send.at[end], row_recv.at[end],
                device(dx, 0), sends, receives,
            )

    quotients_of(0)
    rows_of(0)
    quotients_of(3)
    cols_of(0)
    send_of(0)
    rows_of(5)
    quotients_of(1)
    cols_of(5)
    send_of(5)
    rows_of(1)
    quotients_of(2)
    cols_of(1)
    send_of(1)
    rows_of(2)
    cols_of(2)
    send_of(2)
    rows_of(3)
    cols_of(3)
    send_of(3)
    rows_of(4)
    cols_of(4)
    send_of(4)

    for copy in halo_copies + label_copies + tile_copies:
        copy.wait_send()

    def sides(band, inside):
        for copy in side_copies[band]:
            copy.wait_recv()
        low = side_in[band, 1].astype(F32)
        high = side_in[band, 0].astype(F32)
        return jnp.concatenate([
            jnp.where(jnp.logical_and(left, inside), low, 0.0),
            jnp.where(jnp.logical_and(right, inside), high, 0.0),
        ], axis=1)

    for c in (1, 0, 2, 3):
        rows = slice(16 * c, 16 * c + 16)
        total = center[rows] + sides(c + 1, True)
        if c == 0:
            for copy in sum((side_copies[band] for band in (0, 1, 2, 3, 5)), []):
                copy.wait_send()
            row_copies[1].wait_recv()
            total = total + sides(BANDS - 1, down) + jnp.where(down, row_in[1].astype(F32), 0.0)
        if c == TILE_BANDS - 1:
            row_copies[0].wait_recv()
            total = total + sides(0, up) + jnp.where(up, row_in[0].astype(F32), 0.0)
        out_ref[rows] = est_v[rows] * (total * (1.0 / VIEWS))

    for copy in side_copies[TILE_BANDS] + list(row_copies.values()):
        copy.wait_send()


def body(view_tiles, tile_owner, tile_offset, estimate, spread_taps):
    nx, ny = lax.axis_size("gx"), lax.axis_size("gy")
    vmem = pl.BlockSpec(memory_space=pltpu.VMEM)
    anywhere = pl.BlockSpec(memory_space=pl.ANY)
    dma = pltpu.SemaphoreType.DMA
    return pl.pallas_call(
        lambda *refs: kernel(nx, ny, *refs),
        out_shape=pltpu.VMEM((ROWS, COLS, DEPTH), F32),
        in_specs=[anywhere] * 5,
        out_specs=vmem,
        scratch_shapes=[
            pltpu.VMEM((ROWS, COLS, DEPTH), F32),
            pltpu.VMEM((TILES, COLS, DEPTH), BF16),
            pltpu.VMEM((9 * SLOTS, COLS, DEPTH), BF16),
            pltpu.VMEM((9 * SLOTS, COLS, DEPTH), BF16),
            pltpu.VMEM((XROWS, XCOLS, DEPTH), BF16),
            pltpu.VMEM((XROWS, VIEWS, COLS, DEPTH), BF16),
            pltpu.VMEM((VIEWS, ROWS, COLS, DEPTH), F32),
            pltpu.VMEM((VIEWS, ROWS, COLS, DEPTH), BF16),
            pltpu.VMEM((2, 16, VIEWS, COLS, DEPTH), BF16),
            pltpu.VMEM((ROWS, COLS, DEPTH), F32),
            pltpu.VMEM((BANDS, 2, 16, HALO, DEPTH), BF16),
            pltpu.VMEM((BANDS, 2, 16, HALO, DEPTH), BF16),
            pltpu.VMEM((2, 16, COLS, DEPTH), BF16),
            pltpu.VMEM((2, 16, COLS, DEPTH), BF16),
            pltpu.VMEM((VIEWS, 3, TAPS), F32),
            pltpu.VMEM((TILES,), I32),
            pltpu.VMEM((TILES,), I32),
            pltpu.VMEM((VIEWS, 8, 128), F32),
            pltpu.VMEM((VIEWS, 256, 768), BF16),
            pltpu.VMEM((VIEWS, 256, 768), BF16),
            pltpu.VMEM((VIEWS * COLS, 128), BF16),
            pltpu.VMEM((XCOLS, VIEWS * COLS), BF16),
            pltpu.VMEM((VIEWS // 2, 256, 256), BF16),
            pltpu.VMEM((VIEWS // 2, 256, 256), BF16),
            pltpu.VMEM((8, 128), I32),
            pltpu.SMEM((8, 128), I32),
            pltpu.VMEM((8, 128), I32),
            pltpu.SMEM((8, 128), I32),
            pltpu.VMEM((9, 8, 128), I32),
            pltpu.VMEM((9, 8, 128), I32),
            dma((5,)), dma((2,)), pltpu.SemaphoreType.REGULAR,
            dma((9,)), dma((9,)), dma((9,)), dma((9,)), dma((9,)), dma((9,)),
            dma((BANDS, 2)), dma((BANDS, 2)), dma((2,)), dma((2,)),
        ],
        compiler_params=pltpu.CompilerParams(
            collective_id=0, has_side_effects=True, vmem_limit_bytes=56 * 1024 * 1024
        ),
        name="richardson_lucy",
    )(spread_taps, tile_owner, tile_offset, estimate, view_tiles)


def solution(mesh):
    placed = (
        P(("gx", "gy"), None, None),
        P(("gx", "gy")),
        P(("gx", "gy")),
        P("gx", "gy", None),
        P(),
    )
    return jax.shard_map(
        body, mesh=mesh, in_specs=placed, out_specs=P("gx", "gy", None), check_vma=False
    )
```

```python
import jax
import jax.numpy as jnp
from jax import lax
from jax.experimental import pallas as pl
from jax.experimental.pallas import tpu as pltpu
from jax.sharding import PartitionSpec as P

MESH = pl.DeviceIdType.MESH
F32, BF16, I32 = jnp.float32, jnp.bfloat16, jnp.int32

VIEWS, TAPS = 6, 31
ROWS, COLS, DEPTH = 64, 32, 128
TILES = 384
HALO = 16
XROWS, XCOLS = ROWS + 2 * HALO, COLS + 2 * HALO
SLOTS = 64
WIDE = 640
OWN = 4
ORDER = (8, 6, 2, 0, 7, 1, 5, 3)
BANDS = XROWS // 16
TILE_BANDS = ROWS // 16


def dot(a, b):
    return jnp.dot(a, b, preferred_element_type=F32)


def dot_nt(a, b):
    return lax.dot_general(a, b, (((1,), (1,)), ((), ())), preferred_element_type=F32)


def iota(shape, dim):
    return lax.broadcasted_iota(I32, shape, dim)


def onehot(mask):
    return jnp.where(mask, 1.0, 0.0).astype(BF16)


def shifted_rows(row, rows, shift):
    wide = jnp.broadcast_to(row, (rows, row.shape[1]))
    return pltpu.roll(wide, shift, 1, stride=1, stride_axis=0)


def guarded(condition, action):
    if condition is None:
        action()
    else:
        pl.when(condition)(action)


class Send:
    def __init__(self, src, dst, send_sem, recv_sem, target, sends=None, receives=None):
        self.copy = pltpu.make_async_remote_copy(
            src_ref=src, dst_ref=dst, send_sem=send_sem, recv_sem=recv_sem,
            device_id=target, device_id_type=MESH,
        )
        self.sends, self.receives = sends, receives
        guarded(sends, self.copy.start)

    def wait_recv(self):
        guarded(self.receives, self.copy.wait_recv)

    def wait_send(self):
        guarded(self.sends, self.copy.wait_send)


def lanes(a, b):
    return jnp.concatenate([a, b], axis=1)


def kernel(
    nx, ny,
    taps_hbm, owner_hbm, offset_hbm, est_hbm, tiles_hbm,
    out_ref,
    est_v, tiles_v, packed, arrived, ext, blurred, recip, quot, back_rows,
    center, side_out, side_in, row_out, row_in,
    taps_ref, owner_ref, offset_ref, kpad, row_fwd, row_bwd, col_fwd, col_bwd, depth_fwd, depth_bwd,
    index_v, index_s, slot_v, slot_s, label_out, label_in,
    load_sem, index_sem, relay,
    halo_send, halo_recv, tile_send, tile_recv, label_send, label_recv,
    side_send, side_recv, row_send, row_recv,
):
    gx, gy = lax.axis_index("gx"), lax.axis_index("gy")

    def device(dx, dy):
        return (lax.rem(gx + dx + nx, nx), lax.rem(gy + dy + ny, ny))

    def step_of(group):
        return group // 3 - 1, group % 3 - 1

    barrier = pltpu.get_barrier_semaphore()
    for group in (5, 3, 1, 7):
        pl.semaphore_signal(barrier, inc=1, device_id=device(*step_of(group)), device_id_type=MESH)

    load_est = pltpu.make_async_copy(est_hbm, est_v, load_sem.at[0])
    load_owner = pltpu.make_async_copy(owner_hbm, owner_ref, load_sem.at[2])
    load_offset = pltpu.make_async_copy(offset_hbm, offset_ref, load_sem.at[3])
    load_tiles = pltpu.make_async_copy(tiles_hbm, tiles_v, load_sem.at[1])
    load_taps = pltpu.make_async_copy(taps_hbm, taps_ref, load_sem.at[4])
    load_est.start()
    load_owner.start()
    load_offset.start()
    load_tiles.start()
    load_taps.start()

    load_owner.wait()
    load_offset.wait()
    owner = owner_ref[...].reshape(1, TILES)
    shift = ny.bit_length() - 1

    def wrapped(d, n):
        return jnp.where(d == 0, 1, jnp.where(d == 1, 2, jnp.where(d == 1 - n, 2, 0)))

    group_of = wrapped((owner >> shift) - gx, nx) * 3 + wrapped((owner & (ny - 1)) - gy, ny)
    members = jnp.where(iota((16, TILES), 0) == group_of, 1.0, 0.0)
    before = onehot(iota((TILES, TILES), 0) < iota((TILES, TILES), 1))
    rank = jnp.sum(members * dot(members.astype(BF16), before), axis=0, keepdims=True)
    place = group_of * SLOTS + rank.astype(I32)
    picks = onehot(iota((WIDE, TILES), 0) == place)
    number = iota((8, TILES), 1)
    row = iota((8, TILES), 0)
    offset = jnp.broadcast_to(offset_ref[...].reshape(1, TILES), (8, TILES))
    digits = jnp.where(row == 0, number >> 4, jnp.where(row == 1, number & 15, jnp.where(
        row == 2, offset >> 4, jnp.where(row == 3, offset & 15, 1))))
    found = dot_nt(digits.astype(F32).astype(BF16), picks)
    source = jnp.clip((found[0:1] * 16.0 + found[1:2]).astype(I32), 0, TILES - 1)
    label = (found[2:3] * 16.0 + found[3:4] + (found[4:5] - 1.0) * 1024.0).astype(I32)
    index_v[...] = jnp.zeros_like(index_v)
    for n in range(WIDE // 128):
        index_v[n:n + 1, :] = source[:, n * 128:(n + 1) * 128]
        for group in range(2 * n, min(2 * n + 2, 9)):
            label_out[group] = jnp.broadcast_to(label[:, n * 128:(n + 1) * 128], (8, 128))
    load_index = pltpu.make_async_copy(index_v, index_s, index_sem.at[0])
    load_index.start()

    load_est.wait()
    zero_row = jnp.zeros((XCOLS, DEPTH), BF16)
    ext[0] = zero_row
    ext[XROWS - 1] = zero_row
    ext[HALO:HALO + ROWS, HALO:HALO + COLS, :] = est_v[...].astype(BF16)
    pl.semaphore_wait(barrier, 4)

    up, down, right, left = gx != nx - 1, gx != 0, gy != ny - 1, gy != 0

    def send_halo(group, src, dst, sends, receives):
        return Send(
            ext.at[src], ext.at[dst], halo_send.at[group], halo_recv.at[group],
            device(*step_of(group)), sends, receives,
        )

    inner = slice(HALO, HALO + ROWS)
    halo_copies = [
        send_halo(5, (inner, slice(COLS, COLS + HALO)), (inner, slice(0, HALO)), right, left),
        send_halo(3, (inner, slice(HALO, 2 * HALO)), (inner, slice(HALO + COLS, XCOLS)), left, right),
    ]

    for group in (5, 3):
        pl.semaphore_signal(relay, inc=1, device_id=device(*step_of(group)), device_id_type=MESH)

    label_in[OWN] = label_out[OWN]

    load_index.wait()
    load_tiles.wait()
    tile_copies = []
    away = 2 * (gx % 2) - 1

    def group_at(dx, dy):
        return (dx + 1) * 3 + dy + 1

    def send_tiles(dx, dy):
        group = group_at(dx, dy)

        def pack(r, carry):
            packed[group * SLOTS + r] = tiles_v[index_s[group // 2, group % 2 * SLOTS + r]]
            return carry

        lax.fori_loop(0, SLOTS, pack, 0, unroll=8)
        slots = pl.ds(group * SLOTS, SLOTS)
        tile_copies.append(Send(
            packed.at[slots], arrived.at[slots], tile_send.at[group], tile_recv.at[group], device(dx, dy),
        ))

    pl.semaphore_wait(relay, 2)
    label_copies = [
        Send(
            label_out.at[other], label_in.at[other], label_send.at[other], label_recv.at[other],
            device(*step_of(other)),
        )
        for other in ORDER
    ]
    for dy in (1, -1, 0):
        send_tiles(away, dy)

    def keep(r, carry):
        arrived[OWN * SLOTS + r] = tiles_v[index_s[OWN // 2, OWN % 2 * SLOTS + r]]
        return carry

    lax.fori_loop(0, SLOTS, keep, 0, unroll=8)

    def clear(edge, rows, cols):
        @pl.when(edge)
        def _():
            ext[rows, cols, :] = jnp.zeros((rows.stop - rows.start, cols.stop - cols.start, DEPTH), BF16)

    for copy in halo_copies:
        copy.wait_recv()
    clear(gy == 0, inner, slice(0, HALO))
    clear(gy == ny - 1, inner, slice(HALO + COLS, XCOLS))
    row_halos = [
        send_halo(7, slice(ROWS + 1, ROWS + HALO), slice(1, HALO), up, down),
        send_halo(1, slice(HALO, 2 * HALO - 1), slice(HALO + ROWS, XROWS - 1), down, up),
    ]

    load_taps.wait()
    kpad[...] = jnp.zeros_like(kpad)
    kpad[:, 0:3, 0:TAPS] = taps_ref[...]
    spread = onehot((iota((256, 16), 0) >> 4) == iota((256, 16), 1))
    spread_wide = onehot((iota((768, 128), 0) >> 4) == iota((768, 128), 1))
    same = (iota((256, 256), 0) & 15) == (iota((256, 256), 1) & 15)
    eye = onehot(iota((128, 128), 0) == iota((128, 128), 1))
    depth_fwd[...] = jnp.zeros_like(depth_fwd)
    depth_bwd[...] = jnp.zeros_like(depth_bwd)
    for v in range(VIEWS):
        raw = kpad[v][0:3]
        norm = raw / jnp.sum(raw, axis=1, keepdims=True)
        rows_band = shifted_rows(norm[0:1], 16, 1).astype(BF16)
        wide = dot(spread, rows_band).astype(BF16)
        for d in range(3):
            fwd = dot_nt(wide, spread_wide[256 * d:256 * (d + 1)])
            row_fwd[v, :, 256 * d:256 * (d + 1)] = jnp.where(same, fwd, 0.0).astype(BF16)
            tall = dot_nt(spread_wide[256 * d:256 * (d + 1)], rows_band).astype(BF16)
            bwd = dot_nt(tall, spread)
            row_bwd[v, :, 256 * (2 - d):256 * (3 - d)] = jnp.where(same, bwd, 0.0).astype(BF16)
        cols_band = shifted_rows(norm[1:2], COLS, 1)
        col_fwd[v * COLS:(v + 1) * COLS, :] = cols_band.astype(BF16)
        long = lanes(norm[2:3], jnp.zeros((1, 128), F32))
        depth_t = shifted_rows(long, DEPTH, 128 - TAPS // 2)[:, 128:256].astype(BF16)
        at = slice(128 * (v % 2), 128 * (v % 2) + 128)
        depth_bwd[v // 2, at, at] = depth_t
        depth_fwd[v // 2, at, at] = dot_nt(eye, depth_t).astype(BF16)
    col_bwd[...] = dot_nt(eye[0:XCOLS], col_fwd[...]).astype(BF16)

    for dy in (1, -1, 0):
        send_tiles(-away, dy)
    for dy in (1, -1):
        send_tiles(0, dy)
    for copy in row_halos:
        copy.wait_recv()
    halo_copies += row_halos
    clear(gx == 0, slice(0, HALO), slice(0, XCOLS))
    clear(gx == nx - 1, slice(XROWS - HALO, XROWS), slice(0, XCOLS))

    def columns(p, carry):
        a = 2 * p
        both = lanes(ext[a], ext[a + 1])
        out = dot(col_fwd[:, 0:XCOLS], both).astype(BF16)
        blurred[a] = out[:, 0:128].reshape(VIEWS, COLS, DEPTH)
        blurred[a + 1] = out[:, 128:256].reshape(VIEWS, COLS, DEPTH)
        return carry

    lax.fori_loop(0, XROWS // 2, columns, 0, unroll=8)

    def rows_depth(n, carry):
        band, pair = n // 3, n % 3
        first = pl.multiple_of(band * 16, 16)
        parts = []
        for e in range(2):
            block = blurred[pl.ds(first, 48), 2 * pair + e]
            both = lanes(block[:, 0:16].reshape(768, DEPTH), block[:, 16:32].reshape(768, DEPTH))
            parts.append(dot(row_fwd[2 * pair + e], both).astype(BF16))
        for h in range(2):
            both = lanes(parts[0][:, 128 * h:128 * h + 128], parts[1][:, 128 * h:128 * h + 128])
            inverse = 1.0 / dot(both, depth_fwd[pair])
            for e in range(2):
                recip[2 * pair + e, pl.ds(first, 16), 16 * h:16 * h + 16, :] = inverse[
                    :, 128 * e:128 * e + 128].reshape(16, 16, DEPTH)
        return carry

    lax.fori_loop(0, TILE_BANDS * 3, rows_depth, 0, unroll=3)

    for copy in label_copies:
        copy.wait_recv()
    first_half = iota((1, 128), 1) < SLOTS
    nobody = jnp.full((1, 128), -1, I32)
    labels = jnp.concatenate([
        jnp.where(first_half, label_in[2 * n][0:1], label_in[2 * n + 1][0:1] if 2 * n + 1 < 9 else nobody)
        for n in range(WIDE // 128)
    ], axis=1)
    where_is = onehot(iota((TILES, WIDE), 0) == labels)
    slot_no = iota((8, WIDE), 1)
    slot_digits = jnp.where(iota((8, WIDE), 0) == 0, slot_no >> 4, slot_no & 15)
    got = dot_nt(slot_digits.astype(F32).astype(BF16), where_is)
    slots = jnp.clip((got[0:1] * 16.0 + got[1:2]).astype(I32), 0, 9 * SLOTS - 1)
    slot_v[...] = jnp.zeros_like(slot_v)
    for n in range(3):
        slot_v[n:n + 1, :] = slots[:, 128 * n:128 * (n + 1)]
    load_slots = pltpu.make_async_copy(slot_v, slot_s, index_sem.at[1])
    load_slots.start()
    load_slots.wait()
    for copy in tile_copies:
        copy.wait_recv()

    def quotients_of(band):
        def quotients(pair, carry):
            tiles = []
            for i in range(16):
                halves = []
                for e in range(2):
                    at = slot_s[pair, 64 * e + 16 * band + i]
                    value = arrived[at].astype(F32) * recip[2 * pair + e, 16 * band + i]
                    halves.append(value.astype(BF16))
                tiles.append(lanes(halves[0], halves[1]))
            out = dot(jnp.concatenate(tiles, axis=0), depth_bwd[pair]).astype(BF16)
            for e in range(2):
                quot[2 * pair + e, 16 * band:16 * band + 16] = out[
                    :, 128 * e:128 * e + 128].reshape(16, COLS, DEPTH)
            return carry

        lax.fori_loop(0, 3, quotients, 0, unroll=3)

    def rows_of(band):
        s0, s1 = max(0, band - 2), min(TILE_BANDS - 1, band)
        w0, w1 = 256 * (2 - (band - s0)), 256 * (3 - (band - s1))
        buffer = band % 2

        def rows_back(v, carry):
            block = quot[v, 16 * s0:16 * (s1 + 1)]
            both = lanes(block[:, 0:16].reshape(w1 - w0, DEPTH), block[:, 16:32].reshape(w1 - w0, DEPTH))
            out = dot(row_bwd[v, :, w0:w1], both).astype(BF16)
            back_rows[buffer, :, v, 0:16, :] = out[:, 0:128].reshape(16, 16, DEPTH)
            back_rows[buffer, :, v, 16:32, :] = out[:, 128:256].reshape(16, 16, DEPTH)
            return carry

        lax.fori_loop(0, VIEWS, rows_back, 0, unroll=6)

    def cols_of(band):
        buffer = band % 2

        def cols_back(p, carry):
            both = lanes(
                back_rows[buffer, 2 * p].reshape(VIEWS * COLS, DEPTH),
                back_rows[buffer, 2 * p + 1].reshape(VIEWS * COLS, DEPTH),
            )
            out = dot(col_bwd[...], both)
            for e in range(2):
                one = out[:, 128 * e:128 * e + 128]
                side_out[band, 0, 2 * p + e] = one[0:HALO].astype(BF16)
                side_out[band, 1, 2 * p + e] = one[HALO + COLS:XCOLS].astype(BF16)
                mid = one[HALO:HALO + COLS]
                if 1 <= band <= TILE_BANDS:
                    center[16 * (band - 1) + 2 * p + e] = mid
                else:
                    row_out[band // (BANDS - 1), 2 * p + e] = mid.astype(BF16)
            return carry

        lax.fori_loop(0, 8, cols_back, 0, unroll=8)

    side_copies, row_copies = {}, {}

    def send_of(band):
        dx = -1 if band == 0 else 1 if band == BANDS - 1 else 0
        sends, receives = {0: (None, None), -1: (down, up), 1: (up, down)}[dx]
        side_copies[band] = []
        for side in range(2):
            out_of, into = (left, right) if side == 0 else (right, left)
            if dx != 0:
                out_of, into = jnp.logical_and(out_of, sends), jnp.logical_and(into, receives)
            side_copies[band].append(Send(
                side_out.at[band, side], side_in.at[band, side],
                side_send.at[band, side], side_recv.at[band, side],
                device(dx, 2 * side - 1), out_of, into,
            ))
        if dx != 0:
            end = band // (BANDS - 1)
            row_copies[end] = Send(
                row_out.at[end], row_in.at[end], row_send.at[end], row_recv.at[end],
                device(dx, 0), sends, receives,
            )

    quotients_of(0)
    rows_of(0)
    quotients_of(1)
    cols_of(0)
    send_of(0)
    rows_of(1)
    quotients_of(2)
    cols_of(1)
    send_of(1)
    rows_of(2)
    quotients_of(3)
    cols_of(2)
    send_of(2)
    rows_of(3)
    cols_of(3)
    send_of(3)
    rows_of(4)
    cols_of(4)
    send_of(4)
    rows_of(5)
    cols_of(5)
    send_of(5)
    for copy in halo_copies + label_copies + tile_copies:
        copy.wait_send()

    def sides(band, inside):
        for copy in side_copies[band]:
            copy.wait_recv()
        low = side_in[band, 1].astype(F32)
        high = side_in[band, 0].astype(F32)
        return jnp.concatenate([
            jnp.where(jnp.logical_and(left, inside), low, 0.0),
            jnp.where(jnp.logical_and(right, inside), high, 0.0),
        ], axis=1)

    for c in (1, 2, 3, 0):
        rows = slice(16 * c, 16 * c + 16)
        total = center[rows] + sides(c + 1, True)
        if c == 0:
            for copy in sum((side_copies[band] for band in range(BANDS - 1)), []):
                copy.wait_send()
            row_copies[1].wait_recv()
            total = total + sides(BANDS - 1, down) + jnp.where(down, row_in[1].astype(F32), 0.0)
        if c == TILE_BANDS - 1:
            row_copies[0].wait_recv()
            total = total + sides(0, up) + jnp.where(up, row_in[0].astype(F32), 0.0)
        out_ref[rows] = est_v[rows] * (total * (1.0 / VIEWS))

    for copy in side_copies[BANDS - 1] + list(row_copies.values()):
        copy.wait_send()


def body(view_tiles, tile_owner, tile_offset, estimate, spread_taps):
    nx, ny = lax.axis_size("gx"), lax.axis_size("gy")
    vmem = pl.BlockSpec(memory_space=pltpu.VMEM)
    anywhere = pl.BlockSpec(memory_space=pl.ANY)
    dma = pltpu.SemaphoreType.DMA
    return pl.pallas_call(
        lambda *refs: kernel(nx, ny, *refs),
        out_shape=pltpu.VMEM((ROWS, COLS, DEPTH), F32),
        in_specs=[anywhere] * 5,
        out_specs=vmem,
        scratch_shapes=[
            pltpu.VMEM((ROWS, COLS, DEPTH), F32),
            pltpu.VMEM((TILES, COLS, DEPTH), BF16),
            pltpu.VMEM((9 * SLOTS, COLS, DEPTH), BF16),
            pltpu.VMEM((9 * SLOTS, COLS, DEPTH), BF16),
            pltpu.VMEM((XROWS, XCOLS, DEPTH), BF16),
            pltpu.VMEM((XROWS, VIEWS, COLS, DEPTH), BF16),
            pltpu.VMEM((VIEWS, ROWS, COLS, DEPTH), F32),
            pltpu.VMEM((VIEWS, ROWS, COLS, DEPTH), BF16),
            pltpu.VMEM((2, 16, VIEWS, COLS, DEPTH), BF16),
            pltpu.VMEM((ROWS, COLS, DEPTH), F32),
            pltpu.VMEM((BANDS, 2, 16, HALO, DEPTH), BF16),
            pltpu.VMEM((BANDS, 2, 16, HALO, DEPTH), BF16),
            pltpu.VMEM((2, 16, COLS, DEPTH), BF16),
            pltpu.VMEM((2, 16, COLS, DEPTH), BF16),
            pltpu.VMEM((VIEWS, 3, TAPS), F32),
            pltpu.VMEM((TILES,), I32),
            pltpu.VMEM((TILES,), I32),
            pltpu.VMEM((VIEWS, 8, 128), F32),
            pltpu.VMEM((VIEWS, 256, 768), BF16),
            pltpu.VMEM((VIEWS, 256, 768), BF16),
            pltpu.VMEM((VIEWS * COLS, 128), BF16),
            pltpu.VMEM((XCOLS, VIEWS * COLS), BF16),
            pltpu.VMEM((VIEWS // 2, 256, 256), BF16),
            pltpu.VMEM((VIEWS // 2, 256, 256), BF16),
            pltpu.VMEM((8, 128), I32),
            pltpu.SMEM((8, 128), I32),
            pltpu.VMEM((8, 128), I32),
            pltpu.SMEM((8, 128), I32),
            pltpu.VMEM((9, 8, 128), I32),
            pltpu.VMEM((9, 8, 128), I32),
            dma((5,)), dma((2,)), pltpu.SemaphoreType.REGULAR,
            dma((9,)), dma((9,)), dma((9,)), dma((9,)), dma((9,)), dma((9,)),
            dma((BANDS, 2)), dma((BANDS, 2)), dma((2,)), dma((2,)),
        ],
        compiler_params=pltpu.CompilerParams(
            collective_id=0, has_side_effects=True, vmem_limit_bytes=56 * 1024 * 1024
        ),
        name="richardson_lucy",
    )(spread_taps, tile_owner, tile_offset, estimate, view_tiles)


def solution(mesh):
    placed = (
        P(("gx", "gy"), None, None),
        P(("gx", "gy")),
        P(("gx", "gy")),
        P("gx", "gy", None),
        P(),
    )
    return jax.shard_map(
        body, mesh=mesh, in_specs=placed, out_specs=P("gx", "gy", None), check_vma=False
    )
```
